256 devices in a mesh: board: 64 (over z, x_hi, y), river: 2 (over core), hand: 2 (over x_lo).
Axes of the slice: x: 4 (x_hi: 2, x_lo: 2; x = x_hi * 2 + x_lo), y: 4, z: 8, core: 2. Of those that a mesh axis runs over, the one named last changes fastest.
Arguments:
- reach_probs: float32 [256, 2, 1326], P('board', None, 'hand'), may hold values from 0 to 1
- turn_cards: int32 [256, 4], P('board'), may hold values from 0 to 51, as said below
- river_cards: int32 [256, 48], P('board', 'river'), may hold values from 0 to 51, as said below
- hand_ranks: int32 [256, 48, 1326], P('board', 'river'), may hold values from 0 to 1325
- pot_chips: int32 [256], P('board'), may hold values from 100 to 399
- bet_chips: int32 [256, 2], P('board'), may hold values from 10 to 299
- regrets_first: float32 [256, 48, 3, 1326], P('board', 'river', None, 'hand'), may hold values from 0.01 to 1
- regrets_second: float32 [256, 48, 4, 1326], P('board', 'river', None, 'hand'), may hold values from 0.01 to 1
Outputs:
- turn_values: float32 [256, 2, 1326], P('board', None, 'hand')
- flop_values: float32 [2, 1326], P(None, 'hand')
- new_regrets_first: float32 [256, 48, 3, 1326], P('board', 'river', None, 'hand')
- new_regrets_second: float32 [256, 48, 4, 1326], P('board', 'river', None, 'hand')
The draws below stay inside these ranges and needn't reach their ends.
Inputs may be any that keep to these rules, and one draw needn't show every extreme that they name: For each turn board, the four turn_cards and the 48 river_cards together name every card of the deck once. `river_cards`: see turn_cards.
All inputs are finite; a program needn't handle non-finite values.
Results may differ from the reference program's by a relative error of at most 0.0003.
Values may be sent and summed in bfloat16 or wider, within the bound.
No kernel may reach another device: no remote copies, remote signals or barrier semaphores. Data moves between devices by JAX's collectives and lax.ppermute only.
A program may use at most 64 MiB of HBM per device.

```python
import math
import jax
import jax.numpy as jnp
import numpy as np
from jax import lax

DECK = 52
HANDS = 1326
RIVERS = 48
TURNS = 256


def card_orders(key):
    keys = jax.random.split(key, TURNS)

    def shuffled(single_key):
        return jax.random.permutation(single_key, DECK)
    return jax.vmap(shuffled)(keys).astype(jnp.int32)


def draw_turn_cards(key, part):
    return card_orders(key)[:, :4]


def draw_river_cards(key, part):
    return card_orders(key)[:, 4:]


def with_ends(drawn, rng, smallest, largest):
    shape = drawn.shape
    place = [jax.random.randint(jax.random.fold_in(rng, axis), (), 0, shape[axis]) for axis in range(len(shape))]
    drawn = drawn.at[tuple(place)].set(smallest)
    longest = shape.index(max(shape))
    place[longest] = (place[longest] + 1) % shape[longest]
    return drawn.at[tuple(place)].set(largest)


def shard_levels(key, shape, shards, least, largest):
    def one(dim, blocks):
        steps = jax.random.uniform(jax.random.fold_in(jax.random.fold_in(key, 6), dim), (blocks,), jnp.float32, least / len(shards), largest / len(shards))
        return jnp.repeat(jnp.exp(steps), shape[dim] // blocks).reshape((-1,) + (1,) * (len(shape) - dim - 1))

    level = one(*shards[0])
    for cut in shards[1:]:
        level = level * one(*cut)
    return level


def setup_inputs(seed: int = 0) -> dict:
    streams_of = jax.random.split(jax.random.key(seed), 9)
    return {
        "reach_probs": jnp.clip(1.0 * jax.random.uniform(streams_of[0], (TURNS, 2, HANDS), jnp.float32) ** shard_levels(streams_of[0], (TURNS, 2, HANDS), ((0, 64), (2, 2)), -0.2, 0.2), 0.0, 1.0),
        "turn_cards": draw_turn_cards(jax.random.fold_in(streams_of[8], 71), 0),
        "river_cards": draw_river_cards(jax.random.fold_in(streams_of[8], 71), 0),
        "hand_ranks": with_ends(jax.random.randint(streams_of[3], (TURNS, RIVERS, HANDS), 0, HANDS), jax.random.fold_in(streams_of[3], 1), 0, HANDS - 1).astype(jnp.int32),
        "pot_chips": with_ends(jax.random.randint(streams_of[4], (TURNS,), 100, 400), jax.random.fold_in(streams_of[4], 1), 100, 399).astype(jnp.int32),
        "bet_chips": with_ends(jax.random.randint(streams_of[5], (TURNS, 2), 10, 300), jax.random.fold_in(streams_of[5], 1), 10, 299).astype(jnp.int32),
        "regrets_first": jnp.clip(jnp.exp(math.log(1.0) - 4.6051702 * jax.random.uniform(streams_of[6], (TURNS, RIVERS, 3, HANDS), jnp.float32) ** shard_levels(streams_of[6], (TURNS, RIVERS, 3, HANDS), ((0, 64), (1, 2), (3, 2)), -0.2, 0.2)), 0.01, 1.0),
        "regrets_second": jnp.clip(jnp.exp(math.log(1.0) - 4.6051702 * jax.random.uniform(streams_of[7], (TURNS, RIVERS, 4, HANDS), jnp.float32) ** shard_levels(streams_of[7], (TURNS, RIVERS, 4, HANDS), ((0, 64), (1, 2), (3, 2)), -0.2, 0.2)), 0.01, 1.0),
    }


def incidence_table():
    lower_card, upper_card = np.triu_indices(DECK, 1)
    card_ids = np.arange(DECK)
    hand_table = (card_ids[None, :] == lower_card[:, None]) | (card_ids[None, :] == upper_card[:, None])
    return jnp.asarray(hand_table.astype(np.float32)).astype(jnp.bfloat16)


def settle(showdown, contact_sums, strategy, call_prob, alive_mask, regrets_first, regrets_second, small_share, large_share):
    oop_check = 0.5 * showdown[..., 0, :]
    oop_small = 0.5 * (contact_sums[..., 0, :] - contact_sums[..., 1, :]) + (0.5 + small_share) * showdown[..., 1, :]
    oop_large = 0.5 * (contact_sums[..., 0, :] - contact_sums[..., 2, :]) + (0.5 + large_share) * showdown[..., 2, :]
    action_values = jnp.stack([oop_check, oop_small, oop_large], axis=-2) * alive_mask[..., None, :]
    oop_values = jnp.sum(strategy * action_values, axis=-2)
    new_first = jnp.maximum(regrets_first + action_values - oop_values[..., None, :], 0.0)
    fold_small = -0.5 * contact_sums[..., 4, :] * alive_mask
    call_small = (0.5 + small_share) * showdown[..., 4, :] * alive_mask
    fold_large = -0.5 * contact_sums[..., 5, :] * alive_mask
    call_large = (0.5 + large_share) * showdown[..., 5, :] * alive_mask
    node_small = (1.0 - call_prob[..., 0, :]) * fold_small + call_prob[..., 0, :] * call_small
    node_large = (1.0 - call_prob[..., 1, :]) * fold_large + call_prob[..., 1, :] * call_large
    ip_values = 0.5 * showdown[..., 3, :] * alive_mask + node_small + node_large
    utility = jnp.stack([fold_small, call_small, fold_large, call_large], axis=-2)
    node_values = jnp.stack([node_small, node_small, node_large, node_large], axis=-2)
    new_second = jnp.maximum(regrets_second + utility - node_values, 0.0)
    return oop_values, ip_values, new_first, new_second


def reference(reach_probs, turn_cards, river_cards, hand_ranks, pot_chips, bet_chips, regrets_first, regrets_second):
    incidence = incidence_table()
    intersection = jnp.dot(incidence, incidence.T, preferred_element_type=jnp.float32)
    compat = (intersection == 0).astype(jnp.bfloat16)
    deck_ids = jnp.arange(DECK, dtype=jnp.int32)
    contract = (((1,), (1,)), ((), ()))

    def one_turn(operands):
        reach_turn, board_turn, river_row, rank_rows, pot_turn, bet_turn, first_turn, second_turn = operands
        dead_turn = jnp.any(board_turn[:, None] == deck_ids[None, :], axis=0)
        dead_cards = (dead_turn[None, :] | (river_row[:, None] == deck_ids[None, :])).astype(jnp.bfloat16)
        alive_mask = (jnp.dot(dead_cards, incidence.T, preferred_element_type=jnp.float32) == 0).astype(jnp.float32)
        scaling = 2.0 / HANDS
        oop_reach = reach_turn[0][None, :] * scaling * alive_mask
        ip_reach = reach_turn[1][None, :] * scaling * alive_mask
        strategy = first_turn / jnp.sum(first_turn, axis=1, keepdims=True)
        call_prob = second_turn[:, 1::2] / (second_turn[:, 0::2] + second_turn[:, 1::2])
        operand_rows = jnp.stack([ip_reach, ip_reach * call_prob[:, 0], ip_reach * call_prob[:, 1],
                                  oop_reach * strategy[:, 0], oop_reach * strategy[:, 1], oop_reach * strategy[:, 2]],
                                 axis=1).astype(jnp.bfloat16)
        contact_sums = lax.dot_general(operand_rows.reshape(RIVERS * 6, HANDS), compat, contract,
                                       preferred_element_type=jnp.float32).reshape(RIVERS, 6, HANDS)

        def per_river(items):
            rank_row, rows_six = items
            above = (rank_row[:, None] > rank_row[None, :]).astype(jnp.bfloat16)
            below = (rank_row[:, None] < rank_row[None, :]).astype(jnp.bfloat16)
            signed = (above - below) * compat
            return lax.dot_general(rows_six, signed, contract, preferred_element_type=jnp.float32)

        showdown = lax.map(per_river, (rank_rows, operand_rows))
        bet_share = bet_turn.astype(jnp.float32) / pot_turn.astype(jnp.float32)
        oop_values, ip_values, new_first, new_second = settle(showdown, contact_sums, strategy, call_prob, alive_mask,
                                                              first_turn, second_turn, bet_share[0], bet_share[1])
        values = jnp.stack([jnp.sum(oop_values, axis=0), jnp.sum(ip_values, axis=0)], axis=0) / RIVERS
        return values, new_first, new_second

    turn_values, new_first, new_second = lax.map(one_turn, (reach_probs, turn_cards, river_cards, hand_ranks, pot_chips,
                                                            bet_chips, regrets_first, regrets_second))
    flop_values = jnp.sum(turn_values, axis=0)
    return turn_values, flop_values, new_first, new_second
```

```python
import functools

import jax
import jax.numpy as jnp
import numpy as np
from jax import lax
from jax.experimental import pallas as pl
from jax.experimental.pallas import tpu as pltpu
from jax.sharding import Mesh
from jax.sharding import PartitionSpec as P

DECK = 52
HANDS = 1326
RIVERS = 48
HALF = HANDS // 2
TILES = 6
WIDTH = TILES * 128
DEPTH = 672
TURNS_HERE = 4
RIVERS_HERE = 24
PAIRS = TURNS_HERE * RIVERS_HERE
UNROLL = 4
VMEM_LIMIT = 56 << 20


def card_tables():
    lower, upper = np.triu_indices(DECK, 1)
    halves = np.full((2, 2, WIDTH), -1, np.int32)
    for half in range(2):
        halves[half, 0, :HALF] = lower[half * HALF : (half + 1) * HALF]
        halves[half, 1, :HALF] = upper[half * HALF : (half + 1) * HALF]
    compat = np.zeros((2, 2, WIDTH, WIDTH), np.float32)
    for own in range(2):
        for slot in range(2):
            other = own ^ slot
            shares = np.zeros((WIDTH, WIDTH), bool)
            for i in range(2):
                for j in range(2):
                    shares |= halves[other, i][:, None] == halves[own, j][None, :]
            compat[own, slot, :HALF, :HALF] = ~shares[:HALF, :HALF]
    return halves, compat


def alive_rows(cards_ref, turn_ref, river_ref, hand, turn):
    low = jnp.where(hand == 0, cards_ref[0, 0:1, :], cards_ref[1, 0:1, :])
    high = jnp.where(hand == 0, cards_ref[0, 1:2, :], cards_ref[1, 1:2, :])
    good = low >= 0
    for k in range(4):
        dead = turn_ref[turn, k]
        good = good & (low != dead) & (high != dead)
    row = jnp.broadcast_to(river_ref[turn : turn + 1, :], (RIVERS_HERE, RIVERS_HERE))
    diagonal = lax.broadcasted_iota(jnp.int32, row.shape, 0) == lax.broadcasted_iota(
        jnp.int32, row.shape, 1
    )
    column = jnp.sum(jnp.where(diagonal, row, 0), axis=1, keepdims=True)
    column = jnp.broadcast_to(column, (RIVERS_HERE, 128))
    low = jnp.broadcast_to(low, column.shape)
    high = jnp.broadcast_to(high, column.shape)
    good = jnp.broadcast_to(good.astype(jnp.int32), column.shape)
    return (good > 0) & (low != column) & (high != column)


def second_rows(flat, turn, b):
    base = turn * RIVERS_HERE * 4 + 2 * b
    fold = flat[pl.ds(base, RIVERS_HERE, stride=4), :]
    call = flat[pl.ds(base + 1, RIVERS_HERE, stride=4), :]
    return fold, call


def operand_kernel(turn_ref, river_ref, cards_ref, reach_ref, first_ref, second_ref, out_ref):
    hand = lax.axis_index("hand")
    flat = second_ref.reshape(PAIRS * 4, 128)
    scaling = 2.0 / HANDS
    for two in range(TURNS_HERE // 2):
        parts = []
        for turn in (2 * two, 2 * two + 1):
            alive = alive_rows(cards_ref, turn_ref, river_ref, hand, turn)
            x = jnp.where(alive, reach_ref[turn, 0:1, :] * scaling, 0.0)
            y = jnp.where(alive, reach_ref[turn, 1:2, :] * scaling, 0.0)
            actions = [first_ref[turn, a] for a in range(3)]
            total = actions[0] + actions[1] + actions[2]
            rows = [y]
            for b in range(2):
                fold, call = second_rows(flat, turn, b)
                rows.append(jnp.where(alive, y * (call / (fold + call)), 0.0))
            for a in range(3):
                rows.append(jnp.where(alive, x * (actions[a] / total), 0.0))
            parts.append(rows)
        for c in range(6):
            both = jnp.concatenate([parts[0][c], parts[1][c]], axis=0)
            start = c * PAIRS + two * 2 * RIVERS_HERE
            out_ref[0, start : start + 2 * RIVERS_HERE, :] = both.astype(jnp.bfloat16)


def ordered(ranks):
    return lax.shift_left((ranks & 127) + 128, lax.shift_right_logical(ranks, 7)).astype(
        jnp.float32
    )


def sums_kernel(
    slot,
    ranks_ref,
    ops_ref,
    table_ref,
    *refs,
):
    if slot == 0:
        start_refs = None
        show_ref, contact_ref = refs[:2]
        refs = refs[2:]
    else:
        start_refs = refs[:2]
        show_ref, contact_ref = refs[2:4]
        refs = refs[4:]
    compat, negative, rows, staged, columns, rolled, wide, sem = refs
    hand = lax.axis_index("hand")
    fetch = pltpu.make_async_copy(table_ref.at[hand, slot], compat, sem)
    fetch.start()

    lower = ordered(ranks_ref[:, :HALF])
    upper = ordered(ranks_ref[:, HALF:])
    rows[...] = jnp.zeros_like(rows)
    staged[...] = jnp.zeros_like(staged)
    rows[:, :HALF] = jnp.where(hand == 0, lower, upper)
    staged[:PAIRS, :HALF] = jnp.where(hand == slot, lower, upper)
    for tile in range(TILES):
        columns[tile * 128 : (tile + 1) * 128, :] = staged[:, tile * 128 : (tile + 1) * 128].T
        wide[tile, : 6 * PAIRS, :] = ops_ref[tile].astype(jnp.float32)
        wide[tile, 6 * PAIRS :, :] = jnp.zeros((2 * PAIRS, 128), jnp.float32)
    fetch.wait()
    negative[...] = -compat[...]

    chunk = 2 * PAIRS
    for m in range(3):
        for n in range(3):
            acc = jnp.zeros((chunk, 256), jnp.float32)
            for k in range(3):
                left = jnp.concatenate(
                    [ops_ref[2 * k + i, m * chunk : (m + 1) * chunk, :] for i in range(2)], axis=1
                )
                acc += jnp.dot(
                    left,
                    compat[k * 256 : (k + 1) * 256, n * 256 : (n + 1) * 256],
                    preferred_element_type=jnp.float32,
                )
            for i in range(2):
                value = acc[:, i * 128 : (i + 1) * 128]
                if start_refs is not None:
                    value = value + start_refs[1][2 * n + i, m * chunk : (m + 1) * chunk, :]
                contact_ref[2 * n + i, m * chunk : (m + 1) * chunk, :] = value

    def group(g, carry):
        rolled[...] = pltpu.roll(columns[...], 128 - g * UNROLL, 1)
        for j in range(UNROLL):
            pair = g * UNROLL + j
            picked = pl.ds(pair, 8, stride=PAIRS)
            left = jnp.concatenate([wide[tile, picked, :] for tile in range(TILES)], axis=1)
            left = left.astype(jnp.bfloat16)
            mine = rows[pl.ds(pair, 1), :].astype(jnp.bfloat16)
            accs = []
            for n in range(3):
                if start_refs is None:
                    accs.append(jnp.zeros((8, 256), jnp.float32))
                else:
                    accs.append(
                        jnp.concatenate(
                            [start_refs[0][2 * n + i, picked, :] for i in range(2)], axis=1
                        )
                    )
            for k in range(3):
                low = k * 256
                size = min(256, DEPTH - low)
                theirs = jnp.broadcast_to(rolled[low : low + size, j : j + 1], (size, 128))
                theirs = theirs.astype(jnp.bfloat16)
                theirs = jnp.concatenate([theirs, theirs], axis=1)
                for n in range(3):
                    lanes = slice(n * 256, (n + 1) * 256)
                    apart = jnp.broadcast_to(mine[:, lanes], (size, 256)) - theirs
                    sign = jnp.minimum(
                        jnp.maximum(apart, negative[low : low + size, lanes]),
                        compat[low : low + size, lanes],
                    )
                    accs[n] += jnp.dot(
                        left[:, low : low + size], sign, preferred_element_type=jnp.float32
                    )
            for n in range(3):
                for i in range(2):
                    show_ref[2 * n + i, picked, :] = accs[n][:, i * 128 : (i + 1) * 128]
        return carry

    lax.fori_loop(0, PAIRS // UNROLL, group, 0)


def settle_kernel(
    turn_ref,
    pot_ref,
    bet_ref,
    river_ref,
    cards_ref,
    first_ref,
    second_ref,
    show_ref,
    contact_ref,
    values_ref,
    new_first_ref,
    new_second_ref,
):
    hand = lax.axis_index("hand")
    flat = second_ref.reshape(PAIRS * 4, 128)
    new_flat = new_second_ref.reshape(PAIRS * 4, 128)
    for turn in range(TURNS_HERE):
        alive = alive_rows(cards_ref, turn_ref, river_ref, hand, turn).astype(jnp.float32)
        pot = jnp.full((1, 128), pot_ref[turn], jnp.int32).astype(jnp.float32)
        share = [
            0.5 + jnp.full((1, 128), bet_ref[turn, b], jnp.int32).astype(jnp.float32) / pot
            for b in range(2)
        ]

        def show(c):
            start = c * PAIRS + turn * RIVERS_HERE
            return show_ref[0, start : start + RIVERS_HERE, :]

        def contact(c):
            start = c * PAIRS + turn * RIVERS_HERE
            return contact_ref[0, start : start + RIVERS_HERE, :]

        base = contact(0)
        utility = [
            0.5 * show(0) * alive,
            (0.5 * (base - contact(1)) + share[0] * show(1)) * alive,
            (0.5 * (base - contact(2)) + share[1] * show(2)) * alive,
        ]
        actions = [first_ref[turn, a] for a in range(3)]
        total = actions[0] + actions[1] + actions[2]
        v1 = (
            actions[0] / total * utility[0]
            + actions[1] / total * utility[1]
            + actions[2] / total * utility[2]
        )
        for a in range(3):
            new_first_ref[turn, a] = jnp.maximum(actions[a] + utility[a] - v1, 0.0)
        v2 = 0.5 * show(3) * alive
        for b in range(2):
            fold, call = second_rows(flat, turn, b)
            prob = call / (fold + call)
            fold_value = -0.5 * contact(4 + b) * alive
            call_value = share[b] * show(4 + b) * alive
            node = (1.0 - prob) * fold_value + prob * call_value
            v2 = v2 + node
            row = turn * RIVERS_HERE * 4 + 2 * b
            new_flat[pl.ds(row, RIVERS_HERE, stride=4), :] = jnp.maximum(
                fold + fold_value - node, 0.0
            )
            new_flat[pl.ds(row + 1, RIVERS_HERE, stride=4), :] = jnp.maximum(
                call + call_value - node, 0.0
            )
        values_ref[turn, 0:1, :] = jnp.sum(v1, axis=0, keepdims=True)
        values_ref[turn, 1:2, :] = jnp.sum(v2, axis=0, keepdims=True)


def whole(space=pltpu.VMEM):
    return pl.BlockSpec(memory_space=space)


def tiled(*shape):
    count = len(shape)
    return pl.BlockSpec(shape + (128,), lambda tile: (0,) * count + (tile,))


def planes(rows):
    return pl.BlockSpec((1, rows, 128), lambda tile: (tile, 0, 0))


def sums(slot, ranks, operands, table, starts):
    return pl.pallas_call(
        functools.partial(sums_kernel, slot),
        out_shape=(
            jax.ShapeDtypeStruct((TILES, 8 * PAIRS, 128), jnp.float32),
            jax.ShapeDtypeStruct((TILES, 6 * PAIRS, 128), jnp.float32),
        ),
        in_specs=[whole(), whole(), whole(pl.ANY)] + [whole()] * len(starts),
        out_specs=(whole(), whole()),
        scratch_shapes=[
            pltpu.VMEM((WIDTH, WIDTH), jnp.bfloat16),
            pltpu.VMEM((WIDTH, WIDTH), jnp.bfloat16),
            pltpu.VMEM((PAIRS, WIDTH), jnp.float32),
            pltpu.VMEM((128, WIDTH), jnp.float32),
            pltpu.VMEM((WIDTH, 128), jnp.float32),
            pltpu.VMEM((WIDTH, 128), jnp.float32),
            pltpu.VMEM((TILES, 8 * PAIRS, 128), jnp.float32),
            pltpu.SemaphoreType.DMA,
        ],
        compiler_params=pltpu.CompilerParams(vmem_limit_bytes=VMEM_LIMIT),
        cost_estimate=pl.CostEstimate(
            flops=2 * PAIRS * 256 * DEPTH * WIDTH, bytes_accessed=1 << 23, transcendentals=0
        ),
    )(ranks, operands, table, *starts)


def swapped(value, axis, size, step):
    return lax.ppermute(value, axis, [(i, i ^ step) for i in range(size)])


def shards(
    reach_probs,
    turn_cards,
    river_cards,
    hand_ranks,
    pot_chips,
    bet_chips,
    regrets_first,
    regrets_second,
):
    halves, compat = card_tables()
    cards = jnp.asarray(halves)
    table = jnp.asarray(compat).astype(jnp.bfloat16)
    ranks = hand_ranks.reshape(PAIRS, HANDS)
    first = jnp.transpose(regrets_first, (0, 2, 1, 3))
    second = regrets_second.reshape(PAIRS, 4, HALF)
    params = pltpu.CompilerParams(vmem_limit_bytes=VMEM_LIMIT)

    operands = pl.pallas_call(
        operand_kernel,
        grid=(TILES,),
        out_shape=jax.ShapeDtypeStruct((TILES, 6 * PAIRS, 128), jnp.bfloat16),
        in_specs=[
            whole(pltpu.SMEM),
            whole(),
            tiled(2, 2),
            tiled(TURNS_HERE, 2),
            tiled(TURNS_HERE, 3, RIVERS_HERE),
            tiled(PAIRS, 4),
        ],
        out_specs=planes(6 * PAIRS),
        compiler_params=params,
        cost_estimate=pl.CostEstimate(flops=1 << 22, bytes_accessed=1 << 22, transcendentals=0),
    )(turn_cards, river_cards, cards, reach_probs, first, second)

    others = swapped(operands, "hand", 2, 1)
    started = sums(0, ranks, operands, table, ())
    show, contact = sums(1, ranks, others, table, started)

    partial, new_first, new_second = pl.pallas_call(
        settle_kernel,
        grid=(TILES,),
        out_shape=(
            jax.ShapeDtypeStruct((TURNS_HERE, 2, HALF), jnp.float32),
            jax.ShapeDtypeStruct(first.shape, jnp.float32),
            jax.ShapeDtypeStruct(second.shape, jnp.float32),
        ),
        in_specs=[
            whole(pltpu.SMEM),
            whole(pltpu.SMEM),
            whole(pltpu.SMEM),
            whole(),
            tiled(2, 2),
            tiled(TURNS_HERE, 3, RIVERS_HERE),
            tiled(PAIRS, 4),
            planes(8 * PAIRS),
            planes(6 * PAIRS),
        ],
        out_specs=(
            tiled(TURNS_HERE, 2),
            tiled(TURNS_HERE, 3, RIVERS_HERE),
            tiled(PAIRS, 4),
        ),
        compiler_params=params,
        cost_estimate=pl.CostEstimate(flops=1 << 23, bytes_accessed=1 << 23, transcendentals=0),
    )(
        turn_cards,
        pot_chips,
        bet_chips,
        river_cards,
        cards,
        first,
        second,
        show,
        contact,
    )

    turn_values = (partial + swapped(partial, "river", 2, 1)) / RIVERS
    flop_values = jnp.sum(turn_values, axis=0)
    for axis, size in (("y", 4), ("xh", 2), ("z", 8)):
        step = 1
        while step < size:
            flop_values = flop_values + swapped(flop_values, axis, size, step)
            step *= 2
    return (
        turn_values,
        flop_values,
        jnp.transpose(new_first, (0, 2, 1, 3)),
        new_second.reshape(regrets_second.shape),
    )


def solution(mesh):
    board = ("z", "xh", "y")
    split = Mesh(mesh.devices.reshape(8, 2, 4, 2, 2), board + ("river", "hand"))
    placed = (
        P(board, None, "hand"),
        P(board, None),
        P(board, "river"),
        P(board, "river", None),
        P(board),
        P(board, None),
        P(board, "river", None, "hand"),
        P(board, "river", None, "hand"),
    )
    return jax.shard_map(
        shards,
        mesh=split,
        in_specs=placed,
        out_specs=(
            P(board, None, "hand"),
            P(None, "hand"),
            P(board, "river", None, "hand"),
            P(board, "river", None, "hand"),
        ),
        check_vma=False,
    )
```

```python
import functools

import jax
import jax.numpy as jnp
import numpy as np
from jax import lax
from jax.experimental import pallas as pl
from jax.experimental.pallas import tpu as pltpu
from jax.sharding import Mesh
from jax.sharding import PartitionSpec as P

DECK = 52
HANDS = 1326
RIVERS = 48
HALF = HANDS // 2
TILES = 6
WIDTH = TILES * 128
DEPTH = 672
TURNS_HERE = 4
RIVERS_HERE = 24
PAIRS = TURNS_HERE * RIVERS_HERE
UNROLL = 32
STEP_TILES = 3
VMEM_LIMIT = 24 << 20
VMEM_ALONE = 56 << 20


def card_tables():
    lower, upper = np.triu_indices(DECK, 1)
    halves = np.full((2, 2, WIDTH), -1, np.int32)
    for half in range(2):
        halves[half, 0, :HALF] = lower[half * HALF : (half + 1) * HALF]
        halves[half, 1, :HALF] = upper[half * HALF : (half + 1) * HALF]
    compat = np.zeros((2, 2, WIDTH, WIDTH), np.float32)
    for own in range(2):
        for slot in range(2):
            other = own ^ slot
            shares = np.zeros((WIDTH, WIDTH), bool)
            for i in range(2):
                for j in range(2):
                    shares |= halves[other, i][:, None] == halves[own, j][None, :]
            compat[own, slot, :HALF, :HALF] = ~shares[:HALF, :HALF]
    return halves, compat


def alive_rows(cards_ref, turn_ref, river_ref, hand, turn):
    low = jnp.where(hand == 0, cards_ref[0, 0:1, :], cards_ref[1, 0:1, :])
    high = jnp.where(hand == 0, cards_ref[0, 1:2, :], cards_ref[1, 1:2, :])
    good = low >= 0
    for k in range(4):
        dead = turn_ref[turn, k]
        good = good & (low != dead) & (high != dead)
    row = jnp.broadcast_to(river_ref[turn : turn + 1, :], (RIVERS_HERE, RIVERS_HERE))
    diagonal = lax.broadcasted_iota(jnp.int32, row.shape, 0) == lax.broadcasted_iota(
        jnp.int32, row.shape, 1
    )
    column = jnp.sum(jnp.where(diagonal, row, 0), axis=1, keepdims=True)
    column = jnp.broadcast_to(column, (RIVERS_HERE, 128))
    low = jnp.broadcast_to(low, column.shape)
    high = jnp.broadcast_to(high, column.shape)
    good = jnp.broadcast_to(good.astype(jnp.int32), column.shape)
    return (good > 0) & (low != column) & (high != column)


def second_rows(flat, turn, b):
    base = turn * RIVERS_HERE * 4 + 2 * b
    fold = flat[pl.ds(base, RIVERS_HERE, stride=4), :]
    call = flat[pl.ds(base + 1, RIVERS_HERE, stride=4), :]
    return fold, call


def operand_kernel(turn_ref, river_ref, *refs):
    hand = lax.axis_index("hand")
    scaling = 2.0 / HANDS
    out_ref = refs[-1]
    for tile in range(STEP_TILES):
        cards_ref, reach_ref, first_ref, second_ref = refs[tile:-1:STEP_TILES]
        flat = second_ref.reshape(PAIRS * 4, 128)
        for two in range(TURNS_HERE // 2):
            parts = []
            for turn in (2 * two, 2 * two + 1):
                alive = alive_rows(cards_ref, turn_ref, river_ref, hand, turn)
                x = jnp.where(alive, reach_ref[turn, 0:1, :] * scaling, 0.0)
                y = jnp.where(alive, reach_ref[turn, 1:2, :] * scaling, 0.0)
                actions = [first_ref[turn, a] for a in range(3)]
                total = actions[0] + actions[1] + actions[2]
                rows = [y]
                for b in range(2):
                    fold, call = second_rows(flat, turn, b)
                    rows.append(jnp.where(alive, y * (call / (fold + call)), 0.0))
                for a in range(3):
                    rows.append(jnp.where(alive, x * (actions[a] / total), 0.0))
                parts.append(rows)
            for c in range(6):
                both = jnp.concatenate([parts[0][c], parts[1][c]], axis=0)
                start = c * PAIRS + two * 2 * RIVERS_HERE
                out_ref[tile, start : start + 2 * RIVERS_HERE, :] = both.astype(jnp.bfloat16)


def ordered(ranks):
    return lax.shift_left((ranks & 127) + 128, lax.shift_right_logical(ranks, 7)).astype(
        jnp.float32
    )


def opposing_sums(slot, ranks_ref, ops_ref, table_ref, show_ref, contact_ref, scratch):
    compat, negative, rows, staged, columns, rolled, wide, sem = scratch
    hand = lax.axis_index("hand")
    fetch = pltpu.make_async_copy(table_ref.at[hand, slot], compat, sem)
    fetch.start()

    lower = ordered(ranks_ref[:, :HALF])
    upper = ordered(ranks_ref[:, HALF:])
    rows[...] = jnp.zeros_like(rows)
    staged[...] = jnp.zeros_like(staged)
    rows[:, :HALF] = jnp.where(hand == 0, lower, upper)
    staged[:PAIRS, :HALF] = jnp.where(hand == slot, lower, upper)
    for tile in range(TILES):
        columns[tile * 128 : (tile + 1) * 128, :] = staged[:, tile * 128 : (tile + 1) * 128].T
        wide[tile, : 6 * PAIRS, :] = ops_ref[tile].astype(jnp.float32)
        wide[tile, 6 * PAIRS :, :] = jnp.zeros((2 * PAIRS, 128), jnp.float32)
    fetch.wait()
    negative[...] = -compat[...]

    chunk = 2 * PAIRS
    for m in range(3):
        for n in range(3):
            acc = jnp.zeros((chunk, 256), jnp.float32)
            for k in range(3):
                left = jnp.concatenate(
                    [ops_ref[2 * k + i, m * chunk : (m + 1) * chunk, :] for i in range(2)], axis=1
                )
                acc += jnp.dot(
                    left,
                    compat[k * 256 : (k + 1) * 256, n * 256 : (n + 1) * 256],
                    preferred_element_type=jnp.float32,
                )
            for i in range(2):
                contact_ref[2 * n + i, m * chunk : (m + 1) * chunk, :] = acc[
                    :, i * 128 : (i + 1) * 128
                ]

    def group(g, carry):
        rolled[...] = pltpu.roll(columns[...], 128 - g * UNROLL, 1)
        for j in range(UNROLL):
            pair = g * UNROLL + j
            picked = pl.ds(pair, 8, stride=PAIRS)
            left = jnp.concatenate([wide[tile, picked, :] for tile in range(TILES)], axis=1)
            left = left.astype(jnp.bfloat16)
            mine = rows[pl.ds(pair, 1), :].astype(jnp.bfloat16)
            accs = [jnp.zeros((8, 256), jnp.float32) for n in range(3)]
            for k in range(3):
                low = k * 256
                size = min(256, DEPTH - low)
                theirs = jnp.broadcast_to(rolled[low : low + size, j : j + 1], (size, 128))
                theirs = theirs.astype(jnp.bfloat16)
                theirs = jnp.concatenate([theirs, theirs], axis=1)
                for n in range(3):
                    lanes = slice(n * 256, (n + 1) * 256)
                    apart = jnp.broadcast_to(mine[:, lanes], (size, 256)) - theirs
                    sign = jnp.minimum(jnp.maximum(apart, jnp.bfloat16(-1)), jnp.bfloat16(1)) * compat[low : low + size, lanes]
                    accs[n] += jnp.dot(
                        left[:, low : low + size], sign, preferred_element_type=jnp.float32
                    )
            for n in range(3):
                for i in range(2):
                    show_ref[2 * n + i, picked, :] = accs[n][:, i * 128 : (i + 1) * 128]
        return carry

    lax.fori_loop(0, PAIRS // UNROLL, group, 0)


def own_kernel(ranks_ref, ops_ref, table_ref, show_ref, contact_ref, *scratch):
    opposing_sums(0, ranks_ref, ops_ref, table_ref, show_ref, contact_ref, scratch)


def final_kernel(
    turn_ref,
    pot_ref,
    bet_ref,
    river_ref,
    cards_ref,
    ranks_ref,
    ops_ref,
    table_ref,
    *refs,
):
    sources = refs[:4]
    values_ref, flop_ref, new_first_ref, new_second_ref = refs[4:8]
    show_other, contact_other, staged_in, staged_out = refs[8:12]
    held = refs[12:16]
    sems = refs[16:20]
    copies = [pltpu.make_async_copy(*each) for each in zip(sources, held, sems)]
    for copy in copies:
        copy.start()
    opposing_sums(1, ranks_ref, ops_ref, table_ref, show_other, contact_other, refs[20:])
    for copy in copies:
        copy.wait()
    show_own, contact_own, first_ref, second_ref = held
    for tile in range(TILES):
        settle(
            tile,
            turn_ref,
            pot_ref,
            bet_ref,
            river_ref,
            cards_ref,
            first_ref,
            second_ref,
            staged_in,
            staged_out,
            show_own.at[tile],
            show_other.at[tile],
            contact_own.at[tile],
            contact_other.at[tile],
            values_ref,
            flop_ref,
            new_first_ref,
            new_second_ref,
        )


def settle(
    tile,
    turn_ref,
    pot_ref,
    bet_ref,
    river_ref,
    cards_ref,
    first_ref,
    second_ref,
    staged_in,
    staged_out,
    show_own,
    show_other,
    contact_own,
    contact_other,
    values_ref,
    flop_ref,
    new_first_ref,
    new_second_ref,
):
    hand = lax.axis_index("hand")
    width = min(128, HALF - tile * 128)
    lanes = slice(tile * 128, tile * 128 + width)
    wide_lanes = slice(tile * 128, (tile + 1) * 128)
    staged_in[:, :, :width] = second_ref[:, :, lanes]
    flat = staged_in.reshape(PAIRS * 4, 128)
    new_flat = staged_out.reshape(PAIRS * 4, 128)
    for turn in range(TURNS_HERE):
        alive = alive_rows(cards_ref.at[:, :, wide_lanes], turn_ref, river_ref, hand, turn)
        alive = alive.astype(jnp.float32)
        pot = jnp.full((1, 128), pot_ref[turn], jnp.int32).astype(jnp.float32)
        share = [
            0.5 + jnp.full((1, 128), bet_ref[b, turn], jnp.int32).astype(jnp.float32) / pot
            for b in range(2)
        ]

        def rows_of(own, other, c):
            start = c * PAIRS + turn * RIVERS_HERE
            here = slice(start, start + RIVERS_HERE)
            return own[here, :] + other[here, :]

        show = functools.partial(rows_of, show_own, show_other)
        contact = functools.partial(rows_of, contact_own, contact_other)
        base = contact(0)
        utility = [
            0.5 * show(0) * alive,
            (0.5 * (base - contact(1)) + share[0] * show(1)) * alive,
            (0.5 * (base - contact(2)) + share[1] * show(2)) * alive,
        ]
        actions = [first_ref[turn, a, :, lanes] for a in range(3)]
        utility = [value[:, :width] for value in utility]
        total = actions[0] + actions[1] + actions[2]
        v1 = (
            actions[0] / total * utility[0]
            + actions[1] / total * utility[1]
            + actions[2] / total * utility[2]
        )
        for a in range(3):
            new_first_ref[turn, a, :, lanes] = jnp.maximum(actions[a] + utility[a] - v1, 0.0)
        v2 = 0.5 * show(3) * alive
        for b in range(2):
            fold, call = second_rows(flat, turn, b)
            prob = call / (fold + call)
            fold_value = -0.5 * contact(4 + b) * alive
            call_value = share[b] * show(4 + b) * alive
            node = (1.0 - prob) * fold_value + prob * call_value
            v2 = v2 + node
            row = turn * RIVERS_HERE * 4 + 2 * b
            new_flat[pl.ds(row, RIVERS_HERE, stride=4), :] = jnp.maximum(
                fold + fold_value - node, 0.0
            )
            new_flat[pl.ds(row + 1, RIVERS_HERE, stride=4), :] = jnp.maximum(
                call + call_value - node, 0.0
            )
        sums = (jnp.sum(v1, axis=0, keepdims=True), jnp.sum(v2, axis=0, keepdims=True)[:, :width])
        for player in range(2):
            values_ref[turn, player : player + 1, lanes] = sums[player]
        totals = sums if turn == 0 else [total + each for total, each in zip(totals, sums)]
    for player in range(2):
        flop_ref[player : player + 1, lanes] = totals[player] * (1.0 / RIVERS)
    new_second_ref[:, :, lanes] = staged_out[:, :, :width]


def whole(space=pltpu.VMEM):
    return pl.BlockSpec(memory_space=space)


def views(*shape):
    count = len(shape)
    return [
        pl.BlockSpec(
            shape + (128,), lambda step, tile=tile: (0,) * count + (step * STEP_TILES + tile,)
        )
        for tile in range(STEP_TILES)
    ]


def sum_scratch():
    return [
        pltpu.VMEM((WIDTH, WIDTH), jnp.bfloat16),
        pltpu.VMEM((WIDTH, WIDTH), jnp.bfloat16),
        pltpu.VMEM((PAIRS, WIDTH), jnp.float32),
        pltpu.VMEM((128, WIDTH), jnp.float32),
        pltpu.VMEM((WIDTH, 128), jnp.float32),
        pltpu.VMEM((WIDTH, 128), jnp.float32),
        pltpu.VMEM((TILES, 8 * PAIRS, 128), jnp.float32),
        pltpu.SemaphoreType.DMA,
    ]


def exchange(value, axis, *pairs):
    return lax.ppermute(value, axis, [p for a, b in pairs for p in ((a, b), (b, a))])


def shards(
    reach_probs,
    turn_cards,
    river_cards,
    hand_ranks,
    pot_chips,
    bet_chips,
    regrets_first,
    regrets_second,
):
    halves, compat = card_tables()
    cards = jnp.asarray(halves)
    table = jnp.asarray(compat).astype(jnp.bfloat16)
    ranks = hand_ranks.reshape(PAIRS, HANDS)
    first = jnp.transpose(regrets_first, (0, 2, 1, 3))
    second = regrets_second.reshape(PAIRS, 4, HALF)
    params = pltpu.CompilerParams(vmem_limit_bytes=VMEM_LIMIT)
    alone = pltpu.CompilerParams(vmem_limit_bytes=VMEM_ALONE)
    sums_cost = pl.CostEstimate(
        flops=2 * PAIRS * 256 * DEPTH * WIDTH, bytes_accessed=1 << 23, transcendentals=0
    )
    show_shape = (TILES, 8 * PAIRS, 128)
    contact_shape = (TILES, 6 * PAIRS, 128)

    operands = pl.pallas_call(
        operand_kernel,
        grid=(TILES // STEP_TILES,),
        out_shape=jax.ShapeDtypeStruct(contact_shape, jnp.bfloat16),
        in_specs=[whole(pltpu.SMEM), whole()]
        + views(2, 2)
        + views(TURNS_HERE, 2)
        + views(TURNS_HERE, 3, RIVERS_HERE)
        + views(PAIRS, 4),
        out_specs=pl.BlockSpec((STEP_TILES, 6 * PAIRS, 128), lambda step: (step, 0, 0)),
        compiler_params=alone,
        cost_estimate=pl.CostEstimate(flops=1 << 22, bytes_accessed=1 << 22, transcendentals=0),
    )(
        turn_cards,
        river_cards,
        *[cards] * STEP_TILES,
        *[reach_probs] * STEP_TILES,
        *[first] * STEP_TILES,
        *[second] * STEP_TILES,
    )

    others = exchange(operands, "hand", (0, 1))
    show, contact = pl.pallas_call(
        own_kernel,
        out_shape=(
            jax.ShapeDtypeStruct(show_shape, jnp.float32),
            jax.ShapeDtypeStruct(contact_shape, jnp.float32),
        ),
        in_specs=[whole(), whole(), whole(pl.ANY)],
        out_specs=(whole(), whole()),
        scratch_shapes=sum_scratch(),
        compiler_params=params,
        cost_estimate=sums_cost,
    )(ranks, operands, table)

    partial, flop_values, new_first, new_second = pl.pallas_call(
        final_kernel,
        out_shape=(
            jax.ShapeDtypeStruct((TURNS_HERE, 2, HALF), jnp.float32),
            jax.ShapeDtypeStruct((2, HALF), jnp.float32),
            jax.ShapeDtypeStruct(first.shape, jnp.float32),
            jax.ShapeDtypeStruct(second.shape, jnp.float32),
        ),
        in_specs=[whole(pltpu.SMEM)] * 3 + [whole()] * 4 + [whole(pl.ANY)] * 5,
        out_specs=(whole(), whole(), whole(), whole()),
        scratch_shapes=[
            pltpu.VMEM(show_shape, jnp.float32),
            pltpu.VMEM(contact_shape, jnp.float32),
            pltpu.VMEM((PAIRS, 4, 128), jnp.float32),
            pltpu.VMEM((PAIRS, 4, 128), jnp.float32),
            pltpu.VMEM(show_shape, jnp.float32),
            pltpu.VMEM(contact_shape, jnp.float32),
            pltpu.VMEM(first.shape, jnp.float32),
            pltpu.VMEM(second.shape, jnp.float32),
        ]
        + [pltpu.SemaphoreType.DMA] * 4
        + sum_scratch(),
        compiler_params=params,
        cost_estimate=sums_cost,
    )(
        turn_cards,
        pot_chips,
        bet_chips.T,
        river_cards,
        cards,
        ranks,
        others,
        table,
        show,
        contact,
        first,
        second,
    )

    for axis, pairs in (
        ("river", ((0, 1),)),
        ("y", ((0, 1), (2, 3))),
        ("y", ((0, 3), (1, 2))),
        ("xh", ((0, 1),)),
        ("z", ((0, 1), (2, 3), (4, 5), (6, 7))),
        ("z", ((1, 2), (3, 4), (5, 6), (7, 0))),
        ("z", ((2, 5), (1, 6), (0, 3), (4, 7))),
    ):
        flop_values = flop_values + exchange(flop_values, axis, *pairs)
    turn_values = (partial + exchange(partial, "river", (0, 1))) / RIVERS
    return (
        turn_values,
        flop_values,
        jnp.transpose(new_first, (0, 2, 1, 3)),
        new_second.reshape(regrets_second.shape),
    )


def solution(mesh):
    board = ("z", "xh", "y")
    split = Mesh(mesh.devices.reshape(8, 2, 4, 2, 2), board + ("river", "hand"))
    placed = (
        P(board, None, "hand"),
        P(board, None),
        P(board, "river"),
        P(board, "river", None),
        P(board),
        P(board, None),
        P(board, "river", None, "hand"),
        P(board, "river", None, "hand"),
    )
    return jax.shard_map(
        shards,
        mesh=split,
        in_specs=placed,
        out_specs=(
            P(board, None, "hand"),
            P(None, "hand"),
            P(board, "river", None, "hand"),
            P(board, "river", None, "hand"),
        ),
        check_vma=False,
    )
```

```python
import functools

import jax
import jax.numpy as jnp
import numpy as np
from jax import lax
from jax.experimental import pallas as pl
from jax.experimental.pallas import tpu as pltpu
from jax.sharding import Mesh
from jax.sharding import PartitionSpec as P

DECK = 52
HANDS = 1326
RIVERS = 48
HALF = HANDS // 2
TILES = 6
WIDTH = TILES * 128
DEPTH = 672
TURNS_HERE = 4
RIVERS_HERE = 24
PAIRS = TURNS_HERE * RIVERS_HERE
UNROLL = 32
STEP_TILES = 3
VMEM_LIMIT = 24 << 20
VMEM_ALONE = 56 << 20


def card_tables():
    lower, upper = np.triu_indices(DECK, 1)
    halves = np.full((2, 2, WIDTH), -1, np.int32)
    for half in range(2):
        halves[half, 0, :HALF] = lower[half * HALF : (half + 1) * HALF]
        halves[half, 1, :HALF] = upper[half * HALF : (half + 1) * HALF]
    compat = np.zeros((2, 2, WIDTH, WIDTH), np.float32)
    for own in range(2):
        for slot in range(2):
            other = own ^ slot
            shares = np.zeros((WIDTH, WIDTH), bool)
            for i in range(2):
                for j in range(2):
                    shares |= halves[other, i][:, None] == halves[own, j][None, :]
            compat[own, slot, :HALF, :HALF] = ~shares[:HALF, :HALF]
    return halves, compat


def alive_rows(cards_ref, turn_ref, river_ref, hand, turn):
    low = jnp.where(hand == 0, cards_ref[0, 0:1, :], cards_ref[1, 0:1, :])
    high = jnp.where(hand == 0, cards_ref[0, 1:2, :], cards_ref[1, 1:2, :])
    good = low >= 0
    for k in range(4):
        dead = turn_ref[turn, k]
        good = good & (low != dead) & (high != dead)
    row = jnp.broadcast_to(river_ref[turn : turn + 1, :], (RIVERS_HERE, RIVERS_HERE))
    diagonal = lax.broadcasted_iota(jnp.int32, row.shape, 0) == lax.broadcasted_iota(
        jnp.int32, row.shape, 1
    )
    column = jnp.sum(jnp.where(diagonal, row, 0), axis=1, keepdims=True)
    column = jnp.broadcast_to(column, (RIVERS_HERE, 128))
    low = jnp.broadcast_to(low, column.shape)
    high = jnp.broadcast_to(high, column.shape)
    good = jnp.broadcast_to(good.astype(jnp.int32), column.shape)
    return (good > 0) & (low != column) & (high != column)


def second_rows(flat, turn, b):
    base = turn * RIVERS_HERE * 4 + 2 * b
    fold = flat[pl.ds(base, RIVERS_HERE, stride=4), :]
    call = flat[pl.ds(base + 1, RIVERS_HERE, stride=4), :]
    return fold, call


def operand_kernel(turn_ref, river_ref, *refs):
    hand = lax.axis_index("hand")
    scaling = 2.0 / HANDS
    out_ref = refs[-1]
    for tile in range(STEP_TILES):
        cards_ref, reach_ref, first_ref, second_ref = refs[tile:-1:STEP_TILES]
        flat = second_ref.reshape(PAIRS * 4, 128)
        for two in range(TURNS_HERE // 2):
            parts = []
            for turn in (2 * two, 2 * two + 1):
                alive = alive_rows(cards_ref, turn_ref, river_ref, hand, turn)
                x = jnp.where(alive, reach_ref[turn, 0:1, :] * scaling, 0.0)
                y = jnp.where(alive, reach_ref[turn, 1:2, :] * scaling, 0.0)
                actions = [first_ref[turn, a] for a in range(3)]
                total = actions[0] + actions[1] + actions[2]
                rows = [y]
                for b in range(2):
                    fold, call = second_rows(flat, turn, b)
                    rows.append(jnp.where(alive, y * (call / (fold + call)), 0.0))
                for a in range(3):
                    rows.append(jnp.where(alive, x * (actions[a] / total), 0.0))
                parts.append(rows)
            for c in range(6):
                both = jnp.concatenate([parts[0][c], parts[1][c]], axis=0)
                start = c * PAIRS + two * 2 * RIVERS_HERE
                out_ref[tile, start : start + 2 * RIVERS_HERE, :] = both.astype(jnp.bfloat16)


def ordered(ranks):
    return lax.shift_left((ranks & 127) + 128, lax.shift_right_logical(ranks, 7)).astype(
        jnp.float32
    )


def opposing_sums(slot, ranks_ref, ops_ref, table_ref, show_ref, contact_ref, scratch):
    compat, rows, staged, columns, rolled, wide, sem = scratch
    hand = lax.axis_index("hand")
    fetch = pltpu.make_async_copy(table_ref.at[hand, slot], compat, sem)
    fetch.start()

    lower = ordered(ranks_ref[:, :HALF])
    upper = ordered(ranks_ref[:, HALF:])
    rows[...] = jnp.zeros_like(rows)
    staged[...] = jnp.zeros_like(staged)
    rows[:, :HALF] = jnp.where(hand == 0, lower, upper)
    staged[:PAIRS, :HALF] = jnp.where(hand == slot, lower, upper)
    for tile in range(TILES):
        columns[tile * 128 : (tile + 1) * 128, :] = staged[:, tile * 128 : (tile + 1) * 128].T
        wide[tile, : 6 * PAIRS, :] = ops_ref[tile].astype(jnp.float32)
        wide[tile, 6 * PAIRS :, :] = jnp.zeros((2 * PAIRS, 128), jnp.float32)
    fetch.wait()

    chunk = 2 * PAIRS
    for m in range(3):
        for n in range(3):
            acc = jnp.zeros((chunk, 256), jnp.float32)
            for k in range(3):
                left = jnp.concatenate(
                    [ops_ref[2 * k + i, m * chunk : (m + 1) * chunk, :] for i in range(2)], axis=1
                )
                acc += jnp.dot(
                    left,
                    compat[k * 256 : (k + 1) * 256, n * 256 : (n + 1) * 256],
                    preferred_element_type=jnp.float32,
                )
            for i in range(2):
                contact_ref[2 * n + i, m * chunk : (m + 1) * chunk, :] = acc[
                    :, i * 128 : (i + 1) * 128
                ]

    def group(g, carry):
        rolled[...] = pltpu.roll(columns[...], 128 - g * UNROLL, 1)
        for j in range(UNROLL):
            pair = g * UNROLL + j
            picked = pl.ds(pair, 8, stride=PAIRS)
            left = jnp.concatenate([wide[tile, picked, :] for tile in range(TILES)], axis=1)
            left = left.astype(jnp.bfloat16)
            mine = rows[pl.ds(pair, 1), :].astype(jnp.bfloat16)
            accs = [jnp.zeros((8, 256), jnp.float32) for n in range(3)]
            for k in range(3):
                low = k * 256
                size = min(256, DEPTH - low)
                theirs = jnp.broadcast_to(rolled[low : low + size, j : j + 1], (size, 128))
                theirs = theirs.astype(jnp.bfloat16)
                theirs = jnp.concatenate([theirs, theirs], axis=1)
                for n in range(3):
                    lanes = slice(n * 256, (n + 1) * 256)
                    apart = jnp.broadcast_to(mine[:, lanes], (size, 256)) - theirs
                    sign = jnp.minimum(jnp.maximum(apart, jnp.bfloat16(-1)), jnp.bfloat16(1)) * compat[low : low + size, lanes]
                    accs[n] += jnp.dot(
                        left[:, low : low + size], sign, preferred_element_type=jnp.float32
                    )
            for n in range(3):
                for i in range(2):
                    show_ref[2 * n + i, picked, :] = accs[n][:, i * 128 : (i + 1) * 128]
        return carry

    lax.fori_loop(0, PAIRS // UNROLL, group, 0)


def own_kernel(ranks_ref, ops_ref, table_ref, show_ref, contact_ref, *scratch):
    opposing_sums(0, ranks_ref, ops_ref, table_ref, show_ref, contact_ref, scratch)


def values_kernel(
    turn_ref,
    pot_ref,
    bet_ref,
    river_ref,
    cards_ref,
    ranks_ref,
    ops_ref,
    table_ref,
    *refs,
):
    sources = refs[:4]
    values_ref, flop_ref, show_other, contact_other, staged = refs[4:9]
    held = refs[9:13]
    sems = refs[13:17]
    copies = [pltpu.make_async_copy(*each) for each in zip(sources, held, sems)]
    for copy in copies:
        copy.start()
    opposing_sums(1, ranks_ref, ops_ref, table_ref, show_other, contact_other, refs[17:])
    for copy in copies:
        copy.wait()
    show_own, contact_own, first_ref, second_ref = held
    for tile in range(TILES):
        settle(
            tile,
            (turn_ref, pot_ref, bet_ref, river_ref, cards_ref, first_ref, second_ref),
            (show_own, show_other, contact_own, contact_other),
            staged,
            (values_ref, flop_ref),
            None,
        )


def regrets_kernel(*refs):
    for tile in range(TILES):
        settle(tile, refs[:7], refs[7:11], refs[13], None, (refs[11], refs[12], refs[14]))


def settle(tile, inputs, sums, staged_in, values, regrets):
    turn_ref, pot_ref, bet_ref, river_ref, cards_ref, first_ref, second_ref = inputs
    show_own, show_other, contact_own, contact_other = [ref.at[tile] for ref in sums]
    hand = lax.axis_index("hand")
    width = min(128, HALF - tile * 128)
    lanes = slice(tile * 128, tile * 128 + width)
    wide_lanes = slice(tile * 128, (tile + 1) * 128)
    staged_in[:, :, :width] = second_ref[:, :, lanes]
    flat = staged_in.reshape(PAIRS * 4, 128)
    if regrets is not None:
        new_first_ref, new_second_ref, staged_out = regrets
        new_flat = staged_out.reshape(PAIRS * 4, 128)
    for turn in range(TURNS_HERE):
        alive = alive_rows(cards_ref.at[:, :, wide_lanes], turn_ref, river_ref, hand, turn)
        alive = alive.astype(jnp.float32)
        pot = jnp.full((1, 128), pot_ref[turn], jnp.int32).astype(jnp.float32)
        share = [
            0.5 + jnp.full((1, 128), bet_ref[b, turn], jnp.int32).astype(jnp.float32) / pot
            for b in range(2)
        ]

        def rows_of(own, other, c):
            start = c * PAIRS + turn * RIVERS_HERE
            here = slice(start, start + RIVERS_HERE)
            return own[here, :] + other[here, :]

        show = functools.partial(rows_of, show_own, show_other)
        contact = functools.partial(rows_of, contact_own, contact_other)
        base = contact(0)
        utility = [
            0.5 * show(0) * alive,
            (0.5 * (base - contact(1)) + share[0] * show(1)) * alive,
            (0.5 * (base - contact(2)) + share[1] * show(2)) * alive,
        ]
        actions = [first_ref[turn, a, :, lanes] for a in range(3)]
        utility = [value[:, :width] for value in utility]
        total = actions[0] + actions[1] + actions[2]
        v1 = (
            actions[0] * utility[0] + actions[1] * utility[1] + actions[2] * utility[2]
        ) / total
        if regrets is not None:
            for a in range(3):
                new_first_ref[turn, a, :, lanes] = jnp.maximum(actions[a] + utility[a] - v1, 0.0)
        v2 = 0.5 * show(3) * alive
        for b in range(2):
            fold, call = second_rows(flat, turn, b)
            prob = call / (fold + call)
            fold_value = -0.5 * contact(4 + b) * alive
            call_value = share[b] * show(4 + b) * alive
            node = (1.0 - prob) * fold_value + prob * call_value
            v2 = v2 + node
            if regrets is None:
                continue
            row = turn * RIVERS_HERE * 4 + 2 * b
            new_flat[pl.ds(row, RIVERS_HERE, stride=4), :] = jnp.maximum(
                fold + fold_value - node, 0.0
            )
            new_flat[pl.ds(row + 1, RIVERS_HERE, stride=4), :] = jnp.maximum(
                call + call_value - node, 0.0
            )
        if values is None:
            continue
        values_ref, flop_ref = values
        summed = (jnp.sum(v1, axis=0, keepdims=True), jnp.sum(v2, axis=0, keepdims=True)[:, :width])
        for player in range(2):
            values_ref[turn, player : player + 1, lanes] = summed[player]
        totals = summed if turn == 0 else [total + each for total, each in zip(totals, summed)]
    for player in range(2 if values is not None else 0):
        flop_ref[player : player + 1, lanes] = totals[player] * (1.0 / RIVERS)
    if regrets is not None:
        new_second_ref[:, :, lanes] = staged_out[:, :, :width]


def whole(space=pltpu.VMEM):
    return pl.BlockSpec(memory_space=space)


def views(*shape):
    count = len(shape)
    return [
        pl.BlockSpec(
            shape + (128,), lambda step, tile=tile: (0,) * count + (step * STEP_TILES + tile,)
        )
        for tile in range(STEP_TILES)
    ]


def sum_scratch():
    return [
        pltpu.VMEM((WIDTH, WIDTH), jnp.bfloat16),
        pltpu.VMEM((PAIRS, WIDTH), jnp.float32),
        pltpu.VMEM((128, WIDTH), jnp.float32),
        pltpu.VMEM((WIDTH, 128), jnp.float32),
        pltpu.VMEM((WIDTH, 128), jnp.float32),
        pltpu.VMEM((TILES, 8 * PAIRS, 128), jnp.float32),
        pltpu.SemaphoreType.DMA,
    ]


def exchange(value, axis, *pairs):
    return lax.ppermute(value, axis, [p for a, b in pairs for p in ((a, b), (b, a))])


def depth_sum(value):
    def routes(first, second):
        return [
            pair
            for i in range(8)
            for pair in (((i + first) % 8 * 2, i * 2), ((i + second) % 8 * 2 + 1, i * 2 + 1))
        ]

    axes = ("z", "river")
    near = lax.ppermute(value, axes, routes(-1, 1))
    three = value + near + exchange(near, "river", (0, 1))
    sent = jnp.where(lax.axis_index("river") == 0, three, value + near)
    far = lax.ppermute(sent, axes, routes(3, -3))
    return three + far + exchange(far, "river", (0, 1))


def shards(
    reach_probs,
    turn_cards,
    river_cards,
    hand_ranks,
    pot_chips,
    bet_chips,
    regrets_first,
    regrets_second,
):
    halves, compat = card_tables()
    cards = jnp.asarray(halves)
    table = jnp.asarray(compat).astype(jnp.bfloat16)
    ranks = hand_ranks.reshape(PAIRS, HANDS)
    first = jnp.transpose(regrets_first, (0, 2, 1, 3))
    second = regrets_second.reshape(PAIRS, 4, HALF)
    params = pltpu.CompilerParams(vmem_limit_bytes=VMEM_LIMIT)
    alone = pltpu.CompilerParams(vmem_limit_bytes=VMEM_ALONE)
    sums_cost = pl.CostEstimate(
        flops=2 * PAIRS * 256 * DEPTH * WIDTH, bytes_accessed=1 << 23, transcendentals=0
    )
    show_shape = (TILES, 8 * PAIRS, 128)
    contact_shape = (TILES, 6 * PAIRS, 128)

    operands = pl.pallas_call(
        operand_kernel,
        grid=(TILES // STEP_TILES,),
        out_shape=jax.ShapeDtypeStruct(contact_shape, jnp.bfloat16),
        in_specs=[whole(pltpu.SMEM), whole()]
        + views(2, 2)
        + views(TURNS_HERE, 2)
        + views(TURNS_HERE, 3, RIVERS_HERE)
        + views(PAIRS, 4),
        out_specs=pl.BlockSpec((STEP_TILES, 6 * PAIRS, 128), lambda step: (step, 0, 0)),
        compiler_params=alone,
        cost_estimate=pl.CostEstimate(flops=1 << 22, bytes_accessed=1 << 22, transcendentals=0),
    )(
        turn_cards,
        river_cards,
        *[cards] * STEP_TILES,
        *[reach_probs] * STEP_TILES,
        *[first] * STEP_TILES,
        *[second] * STEP_TILES,
    )

    others = exchange(operands, "hand", (0, 1))
    show, contact = pl.pallas_call(
        own_kernel,
        out_shape=(
            jax.ShapeDtypeStruct(show_shape, jnp.float32),
            jax.ShapeDtypeStruct(contact_shape, jnp.float32),
        ),
        in_specs=[whole(), whole(), whole(pl.ANY)],
        out_specs=(whole(), whole()),
        scratch_shapes=sum_scratch(),
        compiler_params=params,
        cost_estimate=sums_cost,
    )(ranks, operands, table)

    bets = bet_chips.T
    partial, flop_values, show_other, contact_other = pl.pallas_call(
        values_kernel,
        out_shape=(
            jax.ShapeDtypeStruct((TURNS_HERE, 2, HALF), jnp.float32),
            jax.ShapeDtypeStruct((2, HALF), jnp.float32),
            jax.ShapeDtypeStruct(show_shape, jnp.float32),
            jax.ShapeDtypeStruct(contact_shape, jnp.float32),
        ),
        in_specs=[whole(pltpu.SMEM)] * 3 + [whole()] * 4 + [whole(pl.ANY)] * 5,
        out_specs=(whole(),) * 4,
        scratch_shapes=[
            pltpu.VMEM((PAIRS, 4, 128), jnp.float32),
            pltpu.VMEM(show_shape, jnp.float32),
            pltpu.VMEM(contact_shape, jnp.float32),
            pltpu.VMEM(first.shape, jnp.float32),
            pltpu.VMEM(second.shape, jnp.float32),
        ]
        + [pltpu.SemaphoreType.DMA] * 4
        + sum_scratch(),
        compiler_params=params,
        cost_estimate=sums_cost,
    )(
        turn_cards,
        pot_chips,
        bets,
        river_cards,
        cards,
        ranks,
        others,
        table,
        show,
        contact,
        first,
        second,
    )
    new_first, new_second = pl.pallas_call(
        regrets_kernel,
        out_shape=(
            jax.ShapeDtypeStruct(first.shape, jnp.float32),
            jax.ShapeDtypeStruct(second.shape, jnp.float32),
        ),
        in_specs=[whole(pltpu.SMEM)] * 3 + [whole()] * 8,
        out_specs=(whole(), whole()),
        scratch_shapes=[pltpu.VMEM((PAIRS, 4, 128), jnp.float32)] * 2,
        compiler_params=params,
        cost_estimate=pl.CostEstimate(flops=1 << 23, bytes_accessed=1 << 23, transcendentals=0),
    )(
        turn_cards,
        pot_chips,
        bets,
        river_cards,
        cards,
        first,
        second,
        show,
        show_other,
        contact,
        contact_other,
    )

    flop_values = flop_values + exchange(flop_values, "river", (0, 1))
    flop_values = depth_sum(flop_values)
    for axis, pairs in (
        ("y", ((0, 1), (2, 3))),
        ("y", ((0, 3), (1, 2))),
        ("xh", ((0, 1),)),
    ):
        flop_values = flop_values + exchange(flop_values, axis, *pairs)
    turn_values = (partial + exchange(partial, "river", (0, 1))) / RIVERS
    return (
        turn_values,
        flop_values,
        jnp.transpose(new_first, (0, 2, 1, 3)),
        new_second.reshape(regrets_second.shape),
    )


def solution(mesh):
    board = ("z", "xh", "y")
    split = Mesh(mesh.devices.reshape(8, 2, 4, 2, 2), board + ("river", "hand"))
    placed = (
        P(board, None, "hand"),
        P(board, None),
        P(board, "river"),
        P(board, "river", None),
        P(board),
        P(board, None),
        P(board, "river", None, "hand"),
        P(board, "river", None, "hand"),
    )
    return jax.shard_map(
        shards,
        mesh=split,
        in_specs=placed,
        out_specs=(
            P(board, None, "hand"),
            P(None, "hand"),
            P(board, "river", None, "hand"),
            P(board, "river", None, "hand"),
        ),
        check_vma=False,
    )
```

```python
import functools

import jax
import jax.numpy as jnp
import numpy as np
from jax import lax
from jax.experimental import pallas as pl
from jax.experimental.pallas import tpu as pltpu
from jax.sharding import Mesh
from jax.sharding import PartitionSpec as P

DECK = 52
HANDS = 1326
RIVERS = 48
HALF = HANDS // 2
TILES = 6
WIDTH = TILES * 128
DEPTH = 672
TURNS_HERE = 4
RIVERS_HERE = 24
PAIRS = TURNS_HERE * RIVERS_HERE
UNROLL = 32
STEP_TILES = 3
VMEM_LIMIT = 24 << 20
VMEM_ALONE = 56 << 20


def card_tables():
    lower, upper = np.triu_indices(DECK, 1)
    halves = np.full((2, 2, WIDTH), -1, np.int32)
    for half in range(2):
        halves[half, 0, :HALF] = lower[half * HALF : (half + 1) * HALF]
        halves[half, 1, :HALF] = upper[half * HALF : (half + 1) * HALF]
    compat = np.zeros((2, 2, WIDTH, WIDTH), np.float32)
    for own in range(2):
        for slot in range(2):
            other = own ^ slot
            shares = np.zeros((WIDTH, WIDTH), bool)
            for i in range(2):
                for j in range(2):
                    shares |= halves[other, i][:, None] == halves[own, j][None, :]
            compat[own, slot, :HALF, :HALF] = ~shares[:HALF, :HALF]
    return halves, compat


def river_column(river_ref, turn):
    row = jnp.broadcast_to(river_ref[pl.ds(turn, 1), :], (RIVERS_HERE, RIVERS_HERE))
    diagonal = lax.broadcasted_iota(jnp.int32, row.shape, 0) == lax.broadcasted_iota(
        jnp.int32, row.shape, 1
    )
    column = jnp.sum(jnp.where(diagonal, row, 0), axis=1, keepdims=True)
    return jnp.broadcast_to(column, (RIVERS_HERE, 128))


def alive_rows(cards_ref, turn_ref, column, hand, turn):
    low = jnp.where(hand == 0, cards_ref[0, 0:1, :], cards_ref[1, 0:1, :])
    high = jnp.where(hand == 0, cards_ref[0, 1:2, :], cards_ref[1, 1:2, :])
    for k in range(4):
        dead = turn_ref[turn, k]
        low = jnp.where((low == dead) | (high == dead), -1, low)
    low = jnp.broadcast_to(low, column.shape)
    high = jnp.broadcast_to(high, column.shape)
    return (low >= 0) & (low != column) & (high != column)


def second_rows(flat, turn, b):
    base = turn * RIVERS_HERE * 4 + 2 * b
    fold = flat[pl.ds(base, RIVERS_HERE, stride=4), :]
    call = flat[pl.ds(base + 1, RIVERS_HERE, stride=4), :]
    return fold, call


def operand_kernel(turn_ref, river_ref, *refs):
    hand = lax.axis_index("hand")
    scaling = 2.0 / HANDS
    out_ref = refs[-1]
    columns = [river_column(river_ref, turn) for turn in range(TURNS_HERE)]
    for tile in range(STEP_TILES):
        cards_ref, reach_ref, first_ref, second_ref = refs[tile:-1:STEP_TILES]
        flat = second_ref.reshape(PAIRS * 4, 128)
        for two in range(TURNS_HERE // 2):
            parts = []
            for turn in (2 * two, 2 * two + 1):
                alive = alive_rows(cards_ref, turn_ref, columns[turn], hand, turn)
                x = jnp.where(alive, reach_ref[turn, 0:1, :] * scaling, 0.0)
                y = jnp.where(alive, reach_ref[turn, 1:2, :] * scaling, 0.0)
                actions = [first_ref[turn, a] for a in range(3)]
                total = actions[0] + actions[1] + actions[2]
                rows = [y]
                for b in range(2):
                    fold, call = second_rows(flat, turn, b)
                    rows.append(jnp.where(alive, y * (call / (fold + call)), 0.0))
                for a in range(3):
                    rows.append(jnp.where(alive, x * (actions[a] / total), 0.0))
                parts.append(rows)
            for c in range(6):
                both = jnp.concatenate([parts[0][c], parts[1][c]], axis=0)
                start = c * PAIRS + two * 2 * RIVERS_HERE
                out_ref[tile, start : start + 2 * RIVERS_HERE, :] = both.astype(jnp.bfloat16)


def ordered(ranks):
    return lax.shift_left((ranks & 127) + 128, lax.shift_right_logical(ranks, 7)).astype(
        jnp.float32
    )


def opposing_sums(slot, unroll, ranks_ref, ops_ref, table_ref, contact_ref, scratch, put, before, after):
    compat, rows, staged, columns, rolled, wide, sem = scratch
    hand = lax.axis_index("hand")
    fetch = pltpu.make_async_copy(table_ref.at[hand, slot], compat, sem)
    fetch.start()

    lower = ordered(ranks_ref[:, :HALF])
    upper = ordered(ranks_ref[:, HALF:])
    rows[...] = jnp.zeros_like(rows)
    staged[...] = jnp.zeros_like(staged)
    rows[:, :HALF] = jnp.where(hand == 0, lower, upper)
    staged[:PAIRS, :HALF] = jnp.where(hand == slot, lower, upper)
    for tile in range(TILES):
        columns[tile * 128 : (tile + 1) * 128, :] = staged[:, tile * 128 : (tile + 1) * 128].T
        wide[tile, : 6 * PAIRS, :] = ops_ref[tile].astype(jnp.float32)
        wide[tile, 6 * PAIRS :, :] = jnp.zeros((2 * PAIRS, 128), jnp.float32)
    fetch.wait()

    chunk = 2 * PAIRS
    for m in range(3):
        for n in range(3):
            acc = jnp.zeros((chunk, 256), jnp.float32)
            for k in range(3):
                left = jnp.concatenate(
                    [ops_ref[2 * k + i, m * chunk : (m + 1) * chunk, :] for i in range(2)], axis=1
                )
                acc += jnp.dot(
                    left,
                    compat[k * 256 : (k + 1) * 256, n * 256 : (n + 1) * 256],
                    preferred_element_type=jnp.float32,
                )
            for i in range(2):
                contact_ref[2 * n + i, m * chunk : (m + 1) * chunk, :] = acc[
                    :, i * 128 : (i + 1) * 128
                ]

    def group(g, carry):
        before(g)
        rolled[...] = pltpu.roll(columns[...], 128 - g * unroll, 1)
        for j in range(unroll):
            pair = g * unroll + j
            picked = pl.ds(pair, 8, stride=PAIRS)
            left = jnp.concatenate([wide[tile, picked, :] for tile in range(TILES)], axis=1)
            left = left.astype(jnp.bfloat16)
            mine = rows[pl.ds(pair, 1), :].astype(jnp.bfloat16)
            accs = [jnp.zeros((8, 256), jnp.float32) for n in range(3)]
            for k in range(3):
                low = k * 256
                size = min(256, DEPTH - low)
                theirs = jnp.broadcast_to(rolled[low : low + size, j : j + 1], (size, 128))
                theirs = theirs.astype(jnp.bfloat16)
                theirs = jnp.concatenate([theirs, theirs], axis=1)
                for n in range(3):
                    lanes = slice(n * 256, (n + 1) * 256)
                    apart = jnp.broadcast_to(mine[:, lanes], (size, 256)) - theirs
                    sign = jnp.minimum(jnp.maximum(apart, jnp.bfloat16(-1)), jnp.bfloat16(1)) * compat[low : low + size, lanes]
                    accs[n] += jnp.dot(
                        left[:, low : low + size], sign, preferred_element_type=jnp.float32
                    )
            for n in range(3):
                for i in range(2):
                    put(g, j, 2 * n + i, accs[n][:, i * 128 : (i + 1) * 128])
        after(g)
        return carry

    lax.fori_loop(0, PAIRS // unroll, group, 0)


def own_kernel(ranks_ref, ops_ref, table_ref, show_ref, contact_ref, *scratch):
    def put(g, j, tile, value):
        show_ref[tile, pl.ds(g * UNROLL + j, 8, stride=PAIRS), :] = value

    def nothing(g):
        pass

    opposing_sums(
        0, UNROLL, ranks_ref, ops_ref, table_ref, contact_ref, scratch, put, nothing, nothing
    )


def final_kernel(*refs):
    inputs = refs[:5] + refs[8:10]
    ranks_ref, ops_ref, table_ref, show_own, contact_own = refs[5:8] + refs[10:12]
    values_ref, flop_ref, new_first_ref, new_second_ref = refs[12:16]
    fresh, ready, contact_other, staged_in, staged_out = refs[16:21]
    sums = (show_own, ready, contact_own, contact_other)
    ready[...] = jnp.zeros_like(ready)

    turn_ref, pot_ref, bet_ref, river_ref = inputs[:4]

    def settle_turn(turn):
        column = river_column(river_ref, turn)
        pot = jnp.full((1, 128), pot_ref[turn], jnp.int32).astype(jnp.float32)
        share = [
            0.5 + jnp.full((1, 128), bet_ref[b, turn], jnp.int32).astype(jnp.float32) / pot
            for b in range(2)
        ]
        for tile in range(TILES):
            settle(
                tile,
                turn,
                column,
                share,
                (turn_ref,) + inputs[4:],
                sums,
                (staged_in.at[tile], staged_out.at[tile]),
                (values_ref, new_first_ref, new_second_ref),
            )

    def put(g, j, tile, value):
        fresh[tile, pl.ds(j, 8, stride=RIVERS_HERE), :] = value

    def before(g):
        settle_turn(jnp.maximum(g - 1, 0))

    def after(g):
        ready[...] = fresh[...]

    opposing_sums(
        1, RIVERS_HERE, ranks_ref, ops_ref, table_ref, contact_other, refs[21:], put, before, after
    )
    settle_turn(TURNS_HERE - 1)
    total = values_ref[0]
    for turn in range(1, TURNS_HERE):
        total = total + values_ref[turn]
    flop_ref[...] = total * (1.0 / RIVERS)


def settle(tile, turn, column, share, inputs, sums, staged, outputs):
    turn_ref, cards_ref, first_ref, second_ref = inputs
    show_own, show_other, contact_own, contact_other = [ref.at[tile] for ref in sums]
    staged_in, staged_out = staged
    values_ref, new_first_ref, new_second_ref = outputs
    hand = lax.axis_index("hand")
    width = min(128, HALF - tile * 128)
    lanes = slice(tile * 128, tile * 128 + width)
    wide_lanes = slice(tile * 128, (tile + 1) * 128)
    rivers = pl.ds(turn * RIVERS_HERE, RIVERS_HERE)
    staged_in[:, :, :width] = second_ref[rivers, :, lanes]
    flat = staged_in.reshape(RIVERS_HERE * 4, 128)
    new_flat = staged_out.reshape(RIVERS_HERE * 4, 128)
    alive = alive_rows(cards_ref.at[:, :, wide_lanes], turn_ref, column, hand, turn)
    alive = alive.astype(jnp.float32)

    def rows_of(ref, c):
        start = c * PAIRS + turn * RIVERS_HERE
        return ref[pl.ds(pl.multiple_of(start, 8), RIVERS_HERE), :]

    def show(c):
        return rows_of(show_own, c) + show_other[c * RIVERS_HERE : (c + 1) * RIVERS_HERE, :]

    def contact(c):
        return rows_of(contact_own, c) + rows_of(contact_other, c)

    base = contact(0)
    utility = [
        0.5 * show(0) * alive,
        (0.5 * (base - contact(1)) + share[0] * show(1)) * alive,
        (0.5 * (base - contact(2)) + share[1] * show(2)) * alive,
    ]
    actions = [first_ref[turn, a, :, lanes] for a in range(3)]
    utility = [value[:, :width] for value in utility]
    total = actions[0] + actions[1] + actions[2]
    v1 = (actions[0] * utility[0] + actions[1] * utility[1] + actions[2] * utility[2]) / total
    for a in range(3):
        new_first_ref[turn, a, :, lanes] = jnp.maximum(actions[a] + utility[a] - v1, 0.0)
    v2 = 0.5 * show(3) * alive
    for b in range(2):
        fold, call = second_rows(flat, 0, b)
        prob = call / (fold + call)
        fold_value = -0.5 * contact(4 + b) * alive
        call_value = share[b] * show(4 + b) * alive
        node = (1.0 - prob) * fold_value + prob * call_value
        v2 = v2 + node
        new_flat[pl.ds(2 * b, RIVERS_HERE, stride=4), :] = jnp.maximum(
            fold + fold_value - node, 0.0
        )
        new_flat[pl.ds(2 * b + 1, RIVERS_HERE, stride=4), :] = jnp.maximum(
            call + call_value - node, 0.0
        )
    new_second_ref[rivers, :, lanes] = staged_out[:, :, :width]
    summed = (jnp.sum(v1, axis=0, keepdims=True), jnp.sum(v2, axis=0, keepdims=True)[:, :width])
    for player in range(2):
        values_ref[turn, player : player + 1, lanes] = summed[player]


def whole(space=pltpu.VMEM):
    return pl.BlockSpec(memory_space=space)


def views(*shape):
    count = len(shape)
    return [
        pl.BlockSpec(
            shape + (128,), lambda step, tile=tile: (0,) * count + (step * STEP_TILES + tile,)
        )
        for tile in range(STEP_TILES)
    ]


def sum_scratch():
    return [
        pltpu.VMEM((WIDTH, WIDTH), jnp.bfloat16),
        pltpu.VMEM((PAIRS, WIDTH), jnp.float32),
        pltpu.VMEM((128, WIDTH), jnp.float32),
        pltpu.VMEM((WIDTH, 128), jnp.float32),
        pltpu.VMEM((WIDTH, 128), jnp.float32),
        pltpu.VMEM((TILES, 8 * PAIRS, 128), jnp.float32),
        pltpu.SemaphoreType.DMA,
    ]


def exchange(value, axis, *pairs):
    return lax.ppermute(value, axis, [p for a, b in pairs for p in ((a, b), (b, a))])


def depth_sum(value):
    def routes(first, second):
        return [
            pair
            for i in range(8)
            for pair in (((i + first) % 8 * 2, i * 2), ((i + second) % 8 * 2 + 1, i * 2 + 1))
        ]

    axes = ("z", "river")
    near = lax.ppermute(value, axes, routes(-1, 1))
    three = value + near + exchange(near, "river", (0, 1))
    sent = jnp.where(lax.axis_index("river") == 0, three, value + near)
    far = lax.ppermute(sent, axes, routes(3, -3))
    return three + far + exchange(far, "river", (0, 1))


def shards(
    reach_probs,
    turn_cards,
    river_cards,
    hand_ranks,
    pot_chips,
    bet_chips,
    regrets_first,
    regrets_second,
):
    halves, compat = card_tables()
    cards = jnp.asarray(halves)
    table = jnp.asarray(compat).astype(jnp.bfloat16)
    ranks = hand_ranks.reshape(PAIRS, HANDS)
    first = jnp.transpose(regrets_first, (0, 2, 1, 3))
    second = regrets_second.reshape(PAIRS, 4, HALF)
    params = pltpu.CompilerParams(vmem_limit_bytes=VMEM_LIMIT)
    alone = pltpu.CompilerParams(vmem_limit_bytes=VMEM_ALONE)
    sums_cost = pl.CostEstimate(
        flops=2 * PAIRS * 256 * DEPTH * WIDTH, bytes_accessed=1 << 23, transcendentals=0
    )
    show_shape = (TILES, 8 * PAIRS, 128)
    contact_shape = (TILES, 6 * PAIRS, 128)

    operands = pl.pallas_call(
        operand_kernel,
        grid=(TILES // STEP_TILES,),
        out_shape=jax.ShapeDtypeStruct(contact_shape, jnp.bfloat16),
        in_specs=[whole(pltpu.SMEM), whole()]
        + views(2, 2)
        + views(TURNS_HERE, 2)
        + views(TURNS_HERE, 3, RIVERS_HERE)
        + views(PAIRS, 4),
        out_specs=pl.BlockSpec((STEP_TILES, 6 * PAIRS, 128), lambda step: (step, 0, 0)),
        compiler_params=alone,
        cost_estimate=pl.CostEstimate(flops=1 << 22, bytes_accessed=1 << 22, transcendentals=0),
    )(
        turn_cards,
        river_cards,
        *[cards] * STEP_TILES,
        *[reach_probs] * STEP_TILES,
        *[first] * STEP_TILES,
        *[second] * STEP_TILES,
    )

    others = exchange(operands, "hand", (0, 1))
    show, contact = pl.pallas_call(
        own_kernel,
        out_shape=(
            jax.ShapeDtypeStruct(show_shape, jnp.float32),
            jax.ShapeDtypeStruct(contact_shape, jnp.float32),
        ),
        in_specs=[whole(), whole(), whole(pl.ANY)],
        out_specs=(whole(), whole()),
        scratch_shapes=sum_scratch(),
        compiler_params=params,
        cost_estimate=sums_cost,
    )(ranks, operands, table)

    bets = bet_chips.T
    fresh_shape = (TILES, 8 * RIVERS_HERE, 128)
    staged_shape = (TILES, RIVERS_HERE, 4, 128)
    partial, flop_values, new_first, new_second = pl.pallas_call(
        final_kernel,
        out_shape=(
            jax.ShapeDtypeStruct((TURNS_HERE, 2, HALF), jnp.float32),
            jax.ShapeDtypeStruct((2, HALF), jnp.float32),
            jax.ShapeDtypeStruct(first.shape, jnp.float32),
            jax.ShapeDtypeStruct(second.shape, jnp.float32),
        ),
        in_specs=[whole(pltpu.SMEM)] * 3 + [whole()] * 4 + [whole(pl.ANY)] + [whole()] * 4,
        out_specs=(whole(),) * 4,
        scratch_shapes=[
            pltpu.VMEM(fresh_shape, jnp.float32),
            pltpu.VMEM(fresh_shape, jnp.float32),
            pltpu.VMEM(contact_shape, jnp.float32),
            pltpu.VMEM(staged_shape, jnp.float32),
            pltpu.VMEM(staged_shape, jnp.float32),
        ]
        + sum_scratch(),
        compiler_params=params,
        cost_estimate=sums_cost,
    )(
        turn_cards,
        pot_chips,
        bets,
        river_cards,
        cards,
        ranks,
        others,
        table,
        first,
        second,
        show,
        contact,
    )
    flop_values = flop_values + exchange(flop_values, "river", (0, 1))
    flop_values = depth_sum(flop_values)
    for axis, pairs in (
        ("y", ((0, 1), (2, 3))),
        ("y", ((0, 3), (1, 2))),
        ("xh", ((0, 1),)),
    ):
        flop_values = flop_values + exchange(flop_values, axis, *pairs)
    turn_values = (partial + exchange(partial, "river", (0, 1))) / RIVERS
    return (
        turn_values,
        flop_values,
        jnp.transpose(new_first, (0, 2, 1, 3)),
        new_second.reshape(regrets_second.shape),
    )


def solution(mesh):
    board = ("z", "xh", "y")
    split = Mesh(mesh.devices.reshape(8, 2, 4, 2, 2), board + ("river", "hand"))
    placed = (
        P(board, None, "hand"),
        P(board, None),
        P(board, "river"),
        P(board, "river", None),
        P(board),
        P(board, None),
        P(board, "river", None, "hand"),
        P(board, "river", None, "hand"),
    )
    return jax.shard_map(
        shards,
        mesh=split,
        in_specs=placed,
        out_specs=(
            P(board, None, "hand"),
            P(None, "hand"),
            P(board, "river", None, "hand"),
            P(board, "river", None, "hand"),
        ),
        check_vma=False,
    )
```

```python
import functools

import jax
import jax.numpy as jnp
import numpy as np
from jax import lax
from jax.experimental import pallas as pl
from jax.experimental.pallas import tpu as pltpu
from jax.sharding import Mesh
from jax.sharding import PartitionSpec as P

DECK = 52
HANDS = 1326
RIVERS = 48
HALF = HANDS // 2
TILES = 6
WIDTH = TILES * 128
DEPTH = 672
TURNS_HERE = 4
RIVERS_HERE = 24
PAIRS = TURNS_HERE * RIVERS_HERE
UNROLL = 32
STEP_TILES = 3
VMEM_LIMIT = 24 << 20
VMEM_ALONE = 56 << 20


def card_tables():
    lower, upper = np.triu_indices(DECK, 1)
    halves = np.full((2, 2, WIDTH), -1, np.int32)
    for half in range(2):
        halves[half, 0, :HALF] = lower[half * HALF : (half + 1) * HALF]
        halves[half, 1, :HALF] = upper[half * HALF : (half + 1) * HALF]
    compat = np.zeros((2, 2, WIDTH, WIDTH), np.float32)
    for own in range(2):
        for slot in range(2):
            other = own ^ slot
            shares = np.zeros((WIDTH, WIDTH), bool)
            for i in range(2):
                for j in range(2):
                    shares |= halves[other, i][:, None] == halves[own, j][None, :]
            compat[own, slot, :HALF, :HALF] = ~shares[:HALF, :HALF]
    return halves, compat


def river_column(river_ref, turn):
    row = jnp.broadcast_to(river_ref[pl.ds(turn, 1), :], (RIVERS_HERE, RIVERS_HERE))
    diagonal = lax.broadcasted_iota(jnp.int32, row.shape, 0) == lax.broadcasted_iota(
        jnp.int32, row.shape, 1
    )
    column = jnp.sum(jnp.where(diagonal, row, 0), axis=1, keepdims=True)
    return jnp.broadcast_to(column, (RIVERS_HERE, 128))


def alive_rows(cards_ref, turn_ref, column, hand, turn):
    low = jnp.where(hand == 0, cards_ref[0, 0:1, :], cards_ref[1, 0:1, :])
    high = jnp.where(hand == 0, cards_ref[0, 1:2, :], cards_ref[1, 1:2, :])
    for k in range(4):
        dead = turn_ref[turn, k]
        low = jnp.where((low == dead) | (high == dead), -1, low)
    low = jnp.broadcast_to(low, column.shape)
    high = jnp.broadcast_to(high, column.shape)
    return (low >= 0) & (low != column) & (high != column)


def second_rows(flat, turn, b):
    base = turn * RIVERS_HERE * 4 + 2 * b
    fold = flat[pl.ds(base, RIVERS_HERE, stride=4), :]
    call = flat[pl.ds(base + 1, RIVERS_HERE, stride=4), :]
    return fold, call


def operand_kernel(turn_ref, river_ref, *refs):
    hand = lax.axis_index("hand")
    scaling = 2.0 / HANDS
    out_ref = refs[-1]
    columns = [river_column(river_ref, turn) for turn in range(TURNS_HERE)]
    for tile in range(STEP_TILES):
        cards_ref, reach_ref, first_ref, second_ref = refs[tile:-1:STEP_TILES]
        flat = second_ref.reshape(PAIRS * 4, 128)
        for two in range(TURNS_HERE // 2):
            parts = []
            for turn in (2 * two, 2 * two + 1):
                alive = alive_rows(cards_ref, turn_ref, columns[turn], hand, turn)
                x = jnp.where(alive, reach_ref[turn, 0:1, :] * scaling, 0.0)
                y = jnp.where(alive, reach_ref[turn, 1:2, :] * scaling, 0.0)
                actions = [first_ref[turn, a] for a in range(3)]
                total = actions[0] + actions[1] + actions[2]
                rows = [y]
                for b in range(2):
                    fold, call = second_rows(flat, turn, b)
                    rows.append(jnp.where(alive, y * (call / (fold + call)), 0.0))
                for a in range(3):
                    rows.append(jnp.where(alive, x * (actions[a] / total), 0.0))
                parts.append(rows)
            for c in range(6):
                both = jnp.concatenate([parts[0][c], parts[1][c]], axis=0)
                start = c * PAIRS + two * 2 * RIVERS_HERE
                out_ref[tile, start : start + 2 * RIVERS_HERE, :] = both.astype(jnp.bfloat16)


def ordered(ranks):
    return lax.shift_left((ranks & 127) + 128, lax.shift_right_logical(ranks, 7)).astype(
        jnp.float32
    )


def opposing_sums(slot, unroll, ranks_ref, ops_ref, table_ref, contact_ref, scratch, put, before, after):
    compat, rows, staged, columns, rolled, wide, sem = scratch
    hand = lax.axis_index("hand")
    fetch = pltpu.make_async_copy(table_ref.at[hand, slot], compat, sem)
    fetch.start()

    lower = ordered(ranks_ref[:, :HALF])
    upper = ordered(ranks_ref[:, HALF:])
    rows[...] = jnp.zeros_like(rows)
    staged[...] = jnp.zeros_like(staged)
    rows[:, :HALF] = jnp.where(hand == 0, lower, upper)
    staged[:PAIRS, :HALF] = jnp.where(hand == slot, lower, upper)
    for tile in range(TILES):
        columns[tile * 128 : (tile + 1) * 128, :] = staged[:, tile * 128 : (tile + 1) * 128].T
        wide[tile, : 6 * PAIRS, :] = ops_ref[tile].astype(jnp.float32)
        wide[tile, 6 * PAIRS :, :] = jnp.zeros((2 * PAIRS, 128), jnp.float32)
    fetch.wait()

    chunk = 2 * PAIRS
    for m in range(3):
        for n in range(3):
            acc = jnp.zeros((chunk, 256), jnp.float32)
            for k in range(3):
                left = jnp.concatenate(
                    [ops_ref[2 * k + i, m * chunk : (m + 1) * chunk, :] for i in range(2)], axis=1
                )
                acc += jnp.dot(
                    left,
                    compat[k * 256 : (k + 1) * 256, n * 256 : (n + 1) * 256],
                    preferred_element_type=jnp.float32,
                )
            for i in range(2):
                contact_ref[2 * n + i, m * chunk : (m + 1) * chunk, :] = acc[
                    :, i * 128 : (i + 1) * 128
                ]

    def group(g, carry):
        before(g)
        rolled[...] = pltpu.roll(columns[...], (128 - g * unroll) % 128, 1)
        for j in range(unroll):
            pair = g * unroll + j
            picked = pl.ds(pair, 8, stride=PAIRS)
            left = jnp.concatenate([wide[tile, picked, :] for tile in range(TILES)], axis=1)
            left = left.astype(jnp.bfloat16)
            mine = rows[pl.ds(pair, 1), :].astype(jnp.bfloat16)
            accs = [jnp.zeros((8, 256), jnp.float32) for n in range(3)]
            for k in range(3):
                low = k * 256
                size = min(256, DEPTH - low)
                theirs = jnp.broadcast_to(rolled[low : low + size, j : j + 1], (size, 128))
                theirs = theirs.astype(jnp.bfloat16)
                theirs = jnp.concatenate([theirs, theirs], axis=1)
                for n in range(3):
                    lanes = slice(n * 256, (n + 1) * 256)
                    apart = jnp.broadcast_to(mine[:, lanes], (size, 256)) - theirs
                    sign = jnp.minimum(jnp.maximum(apart, jnp.bfloat16(-1)), jnp.bfloat16(1)) * compat[low : low + size, lanes]
                    accs[n] += jnp.dot(
                        left[:, low : low + size], sign, preferred_element_type=jnp.float32
                    )
            for n in range(3):
                for i in range(2):
                    put(g, j, 2 * n + i, accs[n][:, i * 128 : (i + 1) * 128])
        after(g)
        return carry

    if slot == 0:
        lax.fori_loop(0, PAIRS // unroll, group, 0)
        return
    for g in range(PAIRS // unroll):
        group(g, 0)


def own_kernel(ranks_ref, ops_ref, table_ref, show_ref, contact_ref, *scratch):
    def put(g, j, tile, value):
        show_ref[tile, pl.ds(g * UNROLL + j, 8, stride=PAIRS), :] = value

    def nothing(g):
        pass

    opposing_sums(
        0, UNROLL, ranks_ref, ops_ref, table_ref, contact_ref, scratch, put, nothing, nothing
    )


def final_kernel(*refs):
    inputs = refs[:5] + refs[8:10]
    ranks_ref, ops_ref, table_ref, show_own, contact_own = refs[5:8] + refs[10:12]
    values_ref, flop_ref, new_first_ref, new_second_ref = refs[12:16]
    fresh, ready, contact_other, staged_in, staged_out = refs[16:21]
    sums = (show_own, ready, contact_own, contact_other)

    turn_ref, pot_ref, bet_ref, river_ref = inputs[:4]

    def settle_turn(turn):
        column = river_column(river_ref, turn)
        pot = jnp.full((1, 128), pot_ref[turn], jnp.int32).astype(jnp.float32)
        share = [
            0.5 + jnp.full((1, 128), bet_ref[b, turn], jnp.int32).astype(jnp.float32) / pot
            for b in range(2)
        ]
        for tile in range(TILES):
            settle(
                tile,
                turn,
                column,
                share,
                (turn_ref,) + inputs[4:],
                sums,
                (staged_in.at[tile], staged_out.at[tile]),
                (values_ref, new_first_ref, new_second_ref),
            )

    def put(g, j, tile, value):
        fresh[tile, pl.ds(j, 8, stride=RIVERS_HERE), :] = value

    def before(g):
        if g > 0:
            settle_turn(g - 1)

    def after(g):
        ready[...] = fresh[...]

    opposing_sums(
        1, RIVERS_HERE, ranks_ref, ops_ref, table_ref, contact_other, refs[21:], put, before, after
    )
    settle_turn(TURNS_HERE - 1)
    total = values_ref[0]
    for turn in range(1, TURNS_HERE):
        total = total + values_ref[turn]
    flop_ref[...] = total * (1.0 / RIVERS)


def settle(tile, turn, column, share, inputs, sums, staged, outputs):
    turn_ref, cards_ref, first_ref, second_ref = inputs
    show_own, show_other, contact_own, contact_other = [ref.at[tile] for ref in sums]
    staged_in, staged_out = staged
    values_ref, new_first_ref, new_second_ref = outputs
    hand = lax.axis_index("hand")
    width = min(128, HALF - tile * 128)
    lanes = slice(tile * 128, tile * 128 + width)
    wide_lanes = slice(tile * 128, (tile + 1) * 128)
    rivers = pl.ds(turn * RIVERS_HERE, RIVERS_HERE)
    staged_in[:, :, :width] = second_ref[rivers, :, lanes]
    flat = staged_in.reshape(RIVERS_HERE * 4, 128)
    new_flat = staged_out.reshape(RIVERS_HERE * 4, 128)
    alive = alive_rows(cards_ref.at[:, :, wide_lanes], turn_ref, column, hand, turn)
    alive = alive.astype(jnp.float32)

    def rows_of(ref, c):
        start = c * PAIRS + turn * RIVERS_HERE
        return ref[pl.ds(start, RIVERS_HERE), :]

    def show(c):
        return rows_of(show_own, c) + show_other[c * RIVERS_HERE : (c + 1) * RIVERS_HERE, :]

    def contact(c):
        return rows_of(contact_own, c) + rows_of(contact_other, c)

    base = contact(0)
    utility = [
        0.5 * show(0) * alive,
        (0.5 * (base - contact(1)) + share[0] * show(1)) * alive,
        (0.5 * (base - contact(2)) + share[1] * show(2)) * alive,
    ]
    actions = [first_ref[turn, a, :, lanes] for a in range(3)]
    utility = [value[:, :width] for value in utility]
    total = actions[0] + actions[1] + actions[2]
    v1 = (actions[0] * utility[0] + actions[1] * utility[1] + actions[2] * utility[2]) / total
    for a in range(3):
        new_first_ref[turn, a, :, lanes] = jnp.maximum(actions[a] + utility[a] - v1, 0.0)
    v2 = 0.5 * show(3) * alive
    for b in range(2):
        fold, call = second_rows(flat, 0, b)
        prob = call / (fold + call)
        fold_value = -0.5 * contact(4 + b) * alive
        call_value = share[b] * show(4 + b) * alive
        node = (1.0 - prob) * fold_value + prob * call_value
        v2 = v2 + node
        new_flat[pl.ds(2 * b, RIVERS_HERE, stride=4), :] = jnp.maximum(
            fold + fold_value - node, 0.0
        )
        new_flat[pl.ds(2 * b + 1, RIVERS_HERE, stride=4), :] = jnp.maximum(
            call + call_value - node, 0.0
        )
    new_second_ref[rivers, :, lanes] = staged_out[:, :, :width]
    summed = (jnp.sum(v1, axis=0, keepdims=True), jnp.sum(v2, axis=0, keepdims=True)[:, :width])
    for player in range(2):
        values_ref[turn, player : player + 1, lanes] = summed[player]


def whole(space=pltpu.VMEM):
    return pl.BlockSpec(memory_space=space)


def views(*shape):
    count = len(shape)
    return [
        pl.BlockSpec(
            shape + (128,), lambda step, tile=tile: (0,) * count + (step * STEP_TILES + tile,)
        )
        for tile in range(STEP_TILES)
    ]


def sum_scratch():
    return [
        pltpu.VMEM((WIDTH, WIDTH), jnp.bfloat16),
        pltpu.VMEM((PAIRS, WIDTH), jnp.float32),
        pltpu.VMEM((128, WIDTH), jnp.float32),
        pltpu.VMEM((WIDTH, 128), jnp.float32),
        pltpu.VMEM((WIDTH, 128), jnp.float32),
        pltpu.VMEM((TILES, 8 * PAIRS, 128), jnp.float32),
        pltpu.SemaphoreType.DMA,
    ]


def exchange(value, axis, *pairs):
    return lax.ppermute(value, axis, [p for a, b in pairs for p in ((a, b), (b, a))])


def depth_sum(value):
    def routes(first, second):
        return [
            pair
            for i in range(8)
            for pair in (((i + first) % 8 * 2, i * 2), ((i + second) % 8 * 2 + 1, i * 2 + 1))
        ]

    axes = ("z", "river")
    near = lax.ppermute(value, axes, routes(-1, 1))
    three = value + near + exchange(near, "river", (0, 1))
    sent = jnp.where(lax.axis_index("river") == 0, three, value + near)
    far = lax.ppermute(sent, axes, routes(3, -3))
    return three + far + exchange(far, "river", (0, 1))


def shards(
    reach_probs,
    turn_cards,
    river_cards,
    hand_ranks,
    pot_chips,
    bet_chips,
    regrets_first,
    regrets_second,
):
    halves, compat = card_tables()
    cards = jnp.asarray(halves)
    table = jnp.asarray(compat).astype(jnp.bfloat16)
    ranks = hand_ranks.reshape(PAIRS, HANDS)
    first = jnp.transpose(regrets_first, (0, 2, 1, 3))
    second = regrets_second.reshape(PAIRS, 4, HALF)
    params = pltpu.CompilerParams(vmem_limit_bytes=VMEM_LIMIT)
    alone = pltpu.CompilerParams(vmem_limit_bytes=VMEM_ALONE)
    sums_cost = pl.CostEstimate(
        flops=2 * PAIRS * 256 * DEPTH * WIDTH, bytes_accessed=1 << 23, transcendentals=0
    )
    show_shape = (TILES, 8 * PAIRS, 128)
    contact_shape = (TILES, 6 * PAIRS, 128)

    operands = pl.pallas_call(
        operand_kernel,
        grid=(TILES // STEP_TILES,),
        out_shape=jax.ShapeDtypeStruct(contact_shape, jnp.bfloat16),
        in_specs=[whole(pltpu.SMEM), whole()]
        + views(2, 2)
        + views(TURNS_HERE, 2)
        + views(TURNS_HERE, 3, RIVERS_HERE)
        + views(PAIRS, 4),
        out_specs=pl.BlockSpec((STEP_TILES, 6 * PAIRS, 128), lambda step: (step, 0, 0)),
        compiler_params=alone,
        cost_estimate=pl.CostEstimate(flops=1 << 22, bytes_accessed=1 << 22, transcendentals=0),
    )(
        turn_cards,
        river_cards,
        *[cards] * STEP_TILES,
        *[reach_probs] * STEP_TILES,
        *[first] * STEP_TILES,
        *[second] * STEP_TILES,
    )

    others = exchange(operands, "hand", (0, 1))
    show, contact = pl.pallas_call(
        own_kernel,
        out_shape=(
            jax.ShapeDtypeStruct(show_shape, jnp.float32),
            jax.ShapeDtypeStruct(contact_shape, jnp.float32),
        ),
        in_specs=[whole(), whole(), whole(pl.ANY)],
        out_specs=(whole(), whole()),
        scratch_shapes=sum_scratch(),
        compiler_params=params,
        cost_estimate=sums_cost,
    )(ranks, operands, table)

    bets = bet_chips.T
    fresh_shape = (TILES, 8 * RIVERS_HERE, 128)
    staged_shape = (TILES, RIVERS_HERE, 4, 128)
    partial, flop_values, new_first, new_second = pl.pallas_call(
        final_kernel,
        out_shape=(
            jax.ShapeDtypeStruct((TURNS_HERE, 2, HALF), jnp.float32),
            jax.ShapeDtypeStruct((2, HALF), jnp.float32),
            jax.ShapeDtypeStruct(first.shape, jnp.float32),
            jax.ShapeDtypeStruct(second.shape, jnp.float32),
        ),
        in_specs=[whole(pltpu.SMEM)] * 3 + [whole()] * 4 + [whole(pl.ANY)] + [whole()] * 4,
        out_specs=(whole(),) * 4,
        scratch_shapes=[
            pltpu.VMEM(fresh_shape, jnp.float32),
            pltpu.VMEM(fresh_shape, jnp.float32),
            pltpu.VMEM(contact_shape, jnp.float32),
            pltpu.VMEM(staged_shape, jnp.float32),
            pltpu.VMEM(staged_shape, jnp.float32),
        ]
        + sum_scratch(),
        compiler_params=params,
        cost_estimate=sums_cost,
    )(
        turn_cards,
        pot_chips,
        bets,
        river_cards,
        cards,
        ranks,
        others,
        table,
        first,
        second,
        show,
        contact,
    )
    flop_values = flop_values + exchange(flop_values, "river", (0, 1))
    flop_values = depth_sum(flop_values)
    for axis, pairs in (
        ("y", ((0, 1), (2, 3))),
        ("y", ((0, 3), (1, 2))),
        ("xh", ((0, 1),)),
    ):
        flop_values = flop_values + exchange(flop_values, axis, *pairs)
    turn_values = (partial + exchange(partial, "river", (0, 1))) / RIVERS
    return (
        turn_values,
        flop_values,
        jnp.transpose(new_first, (0, 2, 1, 3)),
        new_second.reshape(regrets_second.shape),
    )


def solution(mesh):
    board = ("z", "xh", "y")
    split = Mesh(mesh.devices.reshape(8, 2, 4, 2, 2), board + ("river", "hand"))
    placed = (
        P(board, None, "hand"),
        P(board, None),
        P(board, "river"),
        P(board, "river", None),
        P(board),
        P(board, None),
        P(board, "river", None, "hand"),
        P(board, "river", None, "hand"),
    )
    return jax.shard_map(
        shards,
        mesh=split,
        in_specs=placed,
        out_specs=(
            P(board, None, "hand"),
            P(None, "hand"),
            P(board, "river", None, "hand"),
            P(board, "river", None, "hand"),
        ),
        check_vma=False,
    )
```
